256 devices in a mesh: row: 16 (over y_lo, z), col: 16 (over x, y_hi, core).
Axes of the slice: x: 4, y: 4 (y_hi: 2, y_lo: 2; y = y_hi * 2 + y_lo), z: 8, core: 2. Of those that a mesh axis runs over, the one named last changes fastest.
Arguments:
- features: bfloat16 [131072, 256], P(('col', 'row')), may hold values from -6 to 6
- weight: bfloat16 [256, 256], replicated, may hold values from -0.375 to 0.375
- cotangent: bfloat16 [131072, 256], P(('row', 'col')), may hold values from -6 to 6
- tiles: bfloat16 [16, 16, 32, 128, 128], P('row', 'col'), as said below
- coords: int32 [16, 16, 2, 32], P('row', 'col'), may hold values from 0 to 63, as said below
Outputs:
- activated: bfloat16 [131072, 256], P(('row', 'col'))
- feature_grad: bfloat16 [131072, 256], P(('col', 'row'))
- weight_grad: float32 [256, 256], replicated
The draws below stay inside these ranges and needn't reach their ends.
Inputs may be any that keep to these rules, and one draw needn't show every extreme that they name: `coords`: each device's tiles lie at distinct positions. `tiles`: entries are zero or positive edge weights.
All inputs are finite; a program needn't handle non-finite values.
Results may differ from the reference program's by a relative error of at most 0.0061.
Values may be sent and summed in bfloat16 or wider, within the bound.
A program may use at most 128 MiB of HBM per device.

```python
import math
import jax
import jax.numpy as jnp
from jax import lax

F = 256
TB = 128
NODES_DEV = 512
TILE_DEV = 32
NODES = 131072
N_ROW = 16
N_COL = 16


def draw_coords(key, part):
    key = jax.random.fold_in(key, 11)
    row_count = NODES_DEV * N_COL // TB
    col_count = NODES_DEV * N_ROW // TB
    device_keys = jax.random.split(key, N_ROW * N_COL)

    def single_device(device_key):
        chosen = jax.random.permutation(device_key, row_count * col_count - 1)[:TILE_DEV - 1]
        return jnp.concatenate([chosen.astype(jnp.int32), jnp.full((1,), row_count * col_count - 1, jnp.int32)])
    positions = jax.vmap(single_device)(device_keys)
    stacked = jnp.stack([positions // col_count, positions % col_count], axis=1)
    return stacked.reshape(N_ROW, N_COL, 2, TILE_DEV).astype(jnp.int32)


def draw_tiles(key, part):
    key = jax.random.fold_in(key, 12)
    pattern_key, value_key = jax.random.split(key)
    shape = (N_ROW, N_COL, TILE_DEV, TB, TB)
    pattern = jax.random.randint(pattern_key, shape, 0, 4) == 0
    factor = (0.25 * TILE_DEV * TB * TB / NODES_DEV) ** (-0.5)
    values = jax.random.uniform(value_key, shape, jnp.float32, 0.5, 1.5) * factor
    return jnp.where(pattern, values, 0.0).astype(jnp.bfloat16)


def level_of(key, shape, cuts, low, high):
    loudness = 1.0
    for position, blocks in cuts:
        steps = jax.random.uniform(jax.random.fold_in(jax.random.fold_in(key, 6), position), (blocks,), jnp.float32, low / len(cuts), high / len(cuts))
        loudness = loudness * jnp.repeat(jnp.exp(steps), shape[position] // blocks).reshape((-1,) + (1,) * (len(shape) - 1 - position))
    return loudness


def noise(own_key, shape, spread, limit, cuts=(), kind=jnp.bfloat16):
    drawn = spread * jax.random.normal(own_key, shape, jnp.float32)
    if cuts:
        drawn = drawn * level_of(own_key, shape, cuts, -0.22, 0.18)
    return jnp.clip(drawn, -limit, limit).astype(kind)


def setup_inputs(seed: int = 0) -> dict:
    splits = jax.random.split(jax.random.key(seed), 6)
    features = noise(splits[0], (NODES, F), 1.0, 6.0, ((0, 256),))
    weight = noise(splits[1], (F, F), F ** -0.5, 0.375)
    cotangent = noise(splits[2], (NODES, F), 1.0, 6.0, ((0, 256),))
    tiles = draw_tiles(jax.random.fold_in(splits[5], 71), 0)
    coords = draw_coords(jax.random.fold_in(splits[5], 71), 0)
    return dict(features=features, weight=weight, cotangent=cotangent, tiles=tiles, coords=coords)


def aggregate(tile_list, targets, sources, source_rows, totals, flip):
    count = tile_list.shape[0]
    group = math.gcd(count, 512)
    steps_total = count // group
    width = tile_list.shape[1]
    stacks = (tile_list.reshape(steps_total, group, width, width), targets.reshape(steps_total, group), sources.reshape(steps_total, group))

    def advance(carry, item):
        blocks_now, target_now, source_now = item
        picked = source_rows[source_now].astype(jnp.float32)
        blocks_now = blocks_now.astype(jnp.float32)
        if flip:
            products = jnp.einsum("gba,gbf->gaf", blocks_now, picked)
        else:
            products = jnp.einsum("gab,gbf->gaf", blocks_now, picked)
        return carry.at[target_now].add(products), None

    carry, unused = lax.scan(advance, totals, stacks)
    return carry


def reference(features, weight, cotangent, tiles, coords):
    row_count = NODES_DEV * N_COL // TB
    col_count = NODES_DEV * N_ROW // TB
    block_total = NODES // TB
    tile_list = tiles.reshape(-1, TB, TB)
    row_base = (jnp.arange(N_ROW, dtype=jnp.int32) * row_count)[:, None, None]
    col_base = (jnp.arange(N_COL, dtype=jnp.int32) * col_count)[None, :, None]
    global_rows = (coords[:, :, 0, :] + row_base).reshape(-1).astype(jnp.int32)
    global_cols = (coords[:, :, 1, :] + col_base).reshape(-1).astype(jnp.int32)
    empty = jnp.zeros((block_total, TB, F), jnp.float32)
    forward = aggregate(tile_list, global_rows, global_cols, features.reshape(block_total, TB, F), empty, False)
    agg_rows = forward.reshape(NODES, F).astype(jnp.bfloat16)
    pre = jnp.dot(agg_rows, weight, preferred_element_type=jnp.float32)
    activated = jax.nn.silu(pre).astype(jnp.bfloat16)
    sigma = jax.nn.sigmoid(pre)
    dpre = (cotangent.astype(jnp.float32) * sigma * (1.0 + pre * (1.0 - sigma))).astype(jnp.bfloat16)
    weight_grad = jnp.dot(agg_rows.T, dpre, preferred_element_type=jnp.float32)
    dagg = jnp.dot(dpre, weight.T, preferred_element_type=jnp.float32).astype(jnp.bfloat16)
    backward = aggregate(tile_list, global_cols, global_rows, dagg.reshape(block_total, TB, F), empty, True)
    feature_grad = backward.reshape(NODES, F).astype(jnp.bfloat16)
    return activated, feature_grad, weight_grad
```

```python
import jax
import jax.numpy as jnp
from jax import lax
from jax.experimental import pallas as pl
from jax.experimental.pallas import tpu as pltpu
from jax.sharding import PartitionSpec as P

MESH = pl.DeviceIdType.MESH
BF = jnp.bfloat16
F32 = jnp.float32
TB = 128
NT = 32
NZ = 8
NX = 4
SLOTS = NT + 1
SEMS = 192


def dot(a, b, da, db):
    return lax.dot_general(a, b, (((da,), (db,)), ((), ())), preferred_element_type=F32)


class Net:
    def __init__(self, send, recv):
        self.send, self.recv, self.used, self.started = send, recv, 0, []

    def copy(self, src, dst, device):
        c = pltpu.make_async_remote_copy(
            src_ref=src,
            dst_ref=dst,
            send_sem=self.send.at[self.used],
            recv_sem=self.recv.at[self.used],
            device_id=device,
            device_id_type=MESH,
        )
        self.used += 1
        c.start()
        self.started.append(c)
        return c

    def finish(self):
        for c in self.started:
            c.wait_send()


def wrap(v, n):
    return lax.rem(v + n, n)


def gather(net, n, k, p, dev, own, slot, fill):
    m = n // 2

    def origin(d, s):
        return wrap(k - s, n) if d == 0 else wrap(k + s, n)

    def side(d):
        return dev(wrap(k + 1, n) if d == 0 else wrap(k - 1, n), p)

    def ring(g, pp, d, s, src=None):
        o = origin(d, s - 1)
        lo, cnt = (0, 4) if s < m else (2 * d, 2)
        src = slot(g, pp, o, lo, cnt) if src is None else src
        return net.copy(src, slot(g, pp, o, lo, cnt), side(d))

    def across(o, lo, cnt, src=None):
        src = slot(1, p, o, lo, cnt) if src is None else src
        return net.copy(src, slot(1, p, o, lo, cnt), dev(k, 1 - p))

    q = 1 - p
    ya = net.copy(own(0), slot(0, p, k, 0, 4), dev(k, q))
    b = [ring(1, p, d, 1, own(1)) for d in (0, 1)]
    a0 = [ring(0, p, d, 1, own(0)) for d in (0, 1)]
    y = [across(k, 0, 4, own(1))]
    fill(0)
    ya.wait_recv()
    a1 = [ring(0, q, d, 1) for d in (0, 1)]
    for s in range(2, m + 1):
        nb, n0, n1 = [], [], []
        for d in (0, 1):
            b[d].wait_recv()
            nb.append(ring(1, p, d, s))
            y.append(across(origin(d, s - 1), 0, 4))
        for d in (0, 1):
            a0[d].wait_recv()
            n0.append(ring(0, p, d, s))
        fill(s - 1)
        for d in (0, 1):
            a1[d].wait_recv()
            n1.append(ring(0, q, d, s))
        b, a0, a1 = nb, n0, n1
    fill(m)
    for d in (0, 1):
        b[d].wait_recv()
        y.append(across(origin(d, m), 2 * d, 2))

    def done_a():
        for c in a0 + a1:
            c.wait_recv()

    def done_b():
        for c in y:
            c.wait_recv()

    return done_a, done_b


def scatter(net, n, k, p, dev, part, bufs, out, fill):
    m = n // 2
    sa, ra, sb, rb, sy, ry, sya, rya = bufs
    q = 1 - p
    both = (0, 1)

    def side(d):
        return dev(wrap(k + 1, n) if d == 0 else wrap(k - 1, n), p)

    def emit(dst, lo, cnt, terms):
        def one(i, unused):
            total = terms[0](i)
            for t in terms[1:]:
                total = total + t(i)
            dst[i] = total.astype(BF)
            return unused

        lax.fori_loop(lo, lo + cnt, one, 0)

    def read(ref):
        return lambda i: ref[i].astype(F32)

    def mine(g, pp, t):
        return lambda i: part(g, pp, t, i)

    def send_y(o):
        emit(sy.at[o], 0, 4, [mine(1, q, wrap(k + o, n))])
        return net.copy(sy.at[o], ry.at[o], dev(k, q))

    def step(src, dst, d, s, terms, before):
        if s == 1:
            lo, cnt = 2 * d, 2
            emit(src, lo, cnt, terms)
            return net.copy(src.at[pl.ds(lo, cnt)], dst.at[pl.ds(lo, cnt)], side(d))
        if s == 2:
            emit(src, 2 * d, 2, terms + [read(before)])
            emit(src, 2 - 2 * d, 2, terms)
        else:
            emit(src, 0, 4, terms + [read(before)])
        return net.copy(src, dst, side(d))

    def offset(d, s):
        return m + 1 - s if d == 0 else (n - (m + 1 - s)) % n

    ys = {m: send_y(m)}
    a, b = {}, {}
    for s in range(1, m + 1):
        for j, pp in ((0, q), (1, p)):
            for d in both:
                if s > 1:
                    a[j, d].wait_recv()
                t = wrap(k + offset(d, s), n)
                a[j, d] = step(
                    sa.at[j, d, s - 1], ra.at[j, d, s - 1], d, s, [mine(0, pp, t)], ra.at[j, d, max(s - 2, 0)]
                )
            if s == 1 and j == 0:
                for e in both:
                    o = offset(e, 2)
                    if o not in ys:
                        ys[o] = send_y(o)
        if s == 1:
            for e in range(3, m + 1):
                for d in both:
                    ys[offset(d, e)] = send_y(offset(d, e))
            ys[0] = send_y(0)
        for d in both:
            o = offset(d, s)
            if not (s == 1 and d == 1):
                ys[o].wait_recv()
            if s > 1:
                b[d].wait_recv()
            t = wrap(k + o, n)
            b[d] = step(
                sb.at[d, s - 1],
                rb.at[d, s - 1],
                d,
                s,
                [mine(1, p, t), read(ry.at[o])],
                rb.at[d, max(s - 2, 0)],
            )
        fill(s)
    for d in both:
        a[0, d].wait_recv()
    emit(sya, 0, 4, [mine(0, q, k), read(ra.at[0, 0, m - 1]), read(ra.at[0, 1, m - 1])])
    ya = net.copy(sya, rya, dev(k, q))
    ys[0].wait_recv()
    for d in both:
        b[d].wait_recv()
    emit(out.at[1], 0, 4, [mine(1, p, k), read(ry.at[0]), read(rb.at[0, m - 1]), read(rb.at[1, m - 1])])
    for d in both:
        a[1, d].wait_recv()
    ya.wait_recv()
    emit(
        out.at[0],
        0,
        4,
        [mine(0, p, k), read(ra.at[1, 0, m - 1]), read(ra.at[1, 1, m - 1]), read(rya)],
    )


def kernel(
    x_ref, w_ref, cot_ref, tiles_ref, idx_ref, act_ref, fg_ref, wg_ref,
    tiles, flipped, idx, xs, g0, g1, sums, aggs, af, dself, dother, dg, fgs, fo,
    fa_s, fa_r, fb_s, fb_r, fy_s, fy_r, fya_s, fya_r,
    ba_s, ba_r, bb_s, bb_r, by_s, by_r, bya_s, bya_r,
    wpart, wpair, wrow, wmine, wcol, wfull,
    local, send, recv,
):
    row, col = lax.axis_index("row"), lax.axis_index("col")
    p, z = lax.div(row, NZ), lax.rem(row, NZ)
    h = lax.rem(col, 2)
    chip = lax.div(col, 2)
    x, u = lax.div(chip, 2), lax.rem(chip, 2)
    other = (row, col + 1 - 2 * h)
    net = Net(send, recv)

    def row_dev(k, pp):
        return (pp * NZ + k, col)

    def col_dev(k, pp):
        return (row, (k * 2 + pp) * 2 + h)

    mates = [(wrap(row + d, 16), col) for d in range(1, 16)]
    chips = [(row, wrap(chip + d, 8) * 2 + h) for d in range(1, 8)]

    barrier = pltpu.get_barrier_semaphore()
    for device in mates + chips + [other]:
        pl.semaphore_signal(barrier, inc=1, device_id=device, device_id_type=MESH)

    mine = pl.ds(pl.multiple_of(h * TB, TB), TB)
    theirs = pl.ds(pl.multiple_of((1 - h) * TB, TB), TB)
    cx = pltpu.make_async_copy(x_ref.at[:, :, mine], xs.at[h], local.at[0])
    ct = pltpu.make_async_copy(tiles_ref, tiles.at[h], local.at[1])
    ci = pltpu.make_async_copy(idx_ref, idx.at[h], local.at[2])
    for c in (cx, ct, ci):
        c.start()
    sums[0] = jnp.zeros((TB, TB), F32)
    sums[SLOTS] = jnp.zeros((TB, TB), F32)
    pl.semaphore_wait(barrier, 23)

    rx = net.copy(x_ref.at[:, :, theirs], xs.at[h], other)
    ri = net.copy(idx_ref, idx.at[h], other)
    rt = net.copy(tiles_ref, tiles.at[h], other)
    cx.wait()
    rx.wait_recv()

    gs = (g0, g1)

    def g_slot(g, pp, k, lo, cnt):
        return gs[g].at[pl.ds((pp * NZ + k) * 4 + lo, cnt)]

    def flip(lo, cnt):
        def one(t, unused):
            for g in (0, 1):
                flipped[g, t] = tiles[g, t].T
            return unused

        lax.fori_loop(lo, lo + cnt, one, 0)

    def fill_first(s):
        if s == 0:
            for g in (0, 1):
                gs[g][pl.ds(row * 4, 4)] = xs[g]
        if s == 1:
            ct.wait()
            ci.wait()
            rt.wait_recv()
            ri.wait_recv()
        if s >= 1:
            flip((s - 1) * 8, 8)

    done_a, done_b = gather(net, NZ, z, p, row_dev, lambda g: xs.at[g], g_slot, fill_first)

    def multiply(g, blocks, source, at):
        def one(t, unused):
            block = blocks[g, idx[g, at, t]]
            product = dot(block, source[idx[g, at + 1, t]], 1, 0)
            keep = idx[g, at + 2, t].astype(F32)
            sums[g * SLOTS + 1 + t] = product + keep * sums[g * SLOTS + t]
            return unused

        lax.fori_loop(0, NT, one, 0, unroll=4)

    done_a()
    multiply(0, tiles, g0, 0)
    done_b()
    multiply(1, tiles, g1, 0)

    def forward_part(g, pp, k, i):
        at = ((k * 2 + pp) * 2 + g) * 4 + i
        return sums[idx[0, 3, at]] + sums[SLOTS + idx[1, 3, at]]

    scatter(
        net, NX, x, u, col_dev, forward_part,
        (fa_s, fa_r, fb_s, fb_r, fy_s, fy_r, fya_s, fya_r), aggs, lambda s: None,
    )
    ra = net.copy(aggs.at[1 - h], af.at[h], other)
    af[h] = aggs[h]
    ra.wait_recv()

    agg = jnp.concatenate([af[0].reshape(512, TB), af[1].reshape(512, TB)], axis=1)
    pre = dot(agg, w_ref[...], 1, 0)
    sigma = jax.nn.sigmoid(pre)
    act_ref[...] = (pre * sigma).astype(BF)
    dpre = (cot_ref[...].astype(F32) * sigma * (1.0 + pre * (1.0 - sigma))).astype(BF)
    dagg = dot(dpre, w_ref[...], 1, 1).astype(BF)
    halves = (dagg[:, :TB].reshape(4, TB, TB), dagg[:, TB:].reshape(4, TB, TB))
    dother[0] = halves[0]
    dother[1] = halves[1]
    rd = net.copy(dother.at[1 - h], dself.at[h], other)
    dself[h] = dother[h]
    wpart[...] = dot(agg, dpre, 0, 0)
    rd.wait_recv()

    def d_slot(g, pp, k, lo, cnt):
        return dg.at[pl.ds(((k * 2 + pp) * 2 + g) * 4 + lo, cnt)]

    weights = {}

    def fill_second(s):
        if s == 0:
            weights[0] = net.copy(
                wpart.at[pl.ds(pl.multiple_of((1 - h) * TB, TB), TB)], wpair, other
            )
            dg[pl.ds(chip * 8, 4)] = dself[0]
            dg[pl.ds(chip * 8 + 4, 4)] = dself[1]
        if s == 1:
            weights[0].wait_recv()
            wpair[...] = wpair[...] + wpart[pl.ds(pl.multiple_of(h * TB, TB), TB)]
        if s == 2:
            weights[1] = [
                net.copy(wpair.at[pl.ds(pl.multiple_of(d[0] * 8, 8), 8)], wrow.at[row], d) for d in mates
            ]
            wrow[row] = wpair[pl.ds(pl.multiple_of(row * 8, 8), 8)]

    done_a, done_b = gather(net, NX, x, u, col_dev, lambda g: dself.at[g], d_slot, fill_second)
    done_a()
    done_b()
    multiply(0, flipped, dg, 4)
    multiply(1, flipped, dg, 4)

    def backward_part(g, pp, k, i):
        return sums[g * SLOTS + idx[g, 7, (pp * NZ + k) * 4 + i]]

    def fill_third(s):
        if s == 1:
            for c in weights[1]:
                c.wait_recv()
            total = wrow[0]
            for i in range(1, 16):
                total = total + wrow[i]
            wmine[...] = total
            wcol[chip] = total
            weights[2] = [net.copy(wmine, wcol.at[chip], d) for d in chips]
        if s == 2:
            for c in weights[2]:
                c.wait_recv()
            total = wcol[0]
            for i in range(1, 8):
                total = total + wcol[i]
            here = pl.ds(pl.multiple_of(h * TB + row * 8, 8), 8)
            wfull[here] = total
            weights[3] = [net.copy(wfull.at[here], wfull.at[here], d) for d in mates]
        if s == 3:
            for c in weights[3]:
                c.wait_recv()
            half = pl.ds(pl.multiple_of(h * TB, TB), TB)
            weights[4] = net.copy(wfull.at[half], wfull.at[half], other)
        if s == 4:
            weights[4].wait_recv()
            wg_ref[...] = wfull[...]

    scatter(
        net, NZ, z, p, row_dev, backward_part,
        (ba_s, ba_r, bb_s, bb_r, by_s, by_r, bya_s, bya_r), fgs, fill_third,
    )
    rf = net.copy(fgs.at[1 - h], fo.at[h], other)
    fo[h] = fgs[h]
    rf.wait_recv()
    fg_ref[:, :TB] = fo[0].reshape(512, TB)
    fg_ref[:, TB:] = fo[1].reshape(512, TB)
    net.finish()


def order_of(targets, sources):
    key = targets * 64 + sources
    rank = jnp.sum((key[None, :] < key[:, None]).astype(jnp.int32), axis=1)
    place = (rank[None, :] == jnp.arange(NT)[:, None]).astype(jnp.int32)
    before = (rank[None, :] == jnp.arange(NT)[:, None] - 1).astype(jnp.int32)
    perm = jnp.sum(place * jnp.arange(NT)[None, :], axis=1)
    source = jnp.sum(place * sources[None, :], axis=1)
    now = jnp.sum(place * targets[None, :], axis=1)
    last = jnp.sum(before * (targets + 1)[None, :], axis=1) - 1
    same = (now == last).astype(jnp.int32)
    blocks = jnp.arange(64)
    upto = jnp.sum((targets[None, :] <= blocks[:, None]).astype(jnp.int32), axis=1)
    found = jnp.max((targets[None, :] == blocks[:, None]).astype(jnp.int32), axis=1)
    wide = lambda v: jnp.pad(v, (0, 128 - v.shape[0]))
    return [wide(perm), wide(source), wide(same), wide(upto * found)]


def body(features, weight, cotangent, tiles, coords):
    rows, cols = coords[0, 0, 0], coords[0, 0, 1]
    idx = jnp.stack(order_of(rows, cols) + order_of(cols, rows)).astype(jnp.int32)
    vmem = pl.BlockSpec(memory_space=pltpu.VMEM)
    hbm = pl.BlockSpec(memory_space=pl.ANY)
    unit = (4, TB, TB)

    def sums_for(n):
        m = n // 2
        return [
            pltpu.VMEM((*s, *unit), BF)
            for s in ((2, 2, m), (2, 2, m), (2, m), (2, m), (n,), (n,), (), ())
        ]

    act, fg, wg = pl.pallas_call(
        kernel,
        out_shape=(
            jax.ShapeDtypeStruct((512, 256), BF),
            jax.ShapeDtypeStruct((512, 256), BF),
            jax.ShapeDtypeStruct((256, 256), F32),
        ),
        in_specs=[hbm, vmem, vmem, hbm, hbm],
        out_specs=(vmem, vmem, vmem),
        scratch_shapes=[
            pltpu.VMEM((2, NT, TB, TB), BF),
            pltpu.VMEM((2, NT, TB, TB), BF),
            pltpu.SMEM((2, 8, 128), jnp.int32),
            pltpu.VMEM((2, *unit), BF),
            pltpu.VMEM((64, TB, TB), BF),
            pltpu.VMEM((64, TB, TB), BF),
            pltpu.VMEM((2 * SLOTS, TB, TB), F32),
            pltpu.VMEM((2, *unit), BF),
            pltpu.VMEM((2, *unit), BF),
            pltpu.VMEM((2, *unit), BF),
            pltpu.VMEM((2, *unit), BF),
            pltpu.VMEM((64, TB, TB), BF),
            pltpu.VMEM((2, *unit), BF),
            pltpu.VMEM((2, *unit), BF),
            *sums_for(NX),
            *sums_for(NZ),
            pltpu.VMEM((256, 256), F32),
            pltpu.VMEM((128, 256), F32),
            pltpu.VMEM((16, 8, 256), F32),
            pltpu.VMEM((8, 256), F32),
            pltpu.VMEM((8, 8, 256), F32),
            pltpu.VMEM((256, 256), F32),
            pltpu.SemaphoreType.DMA((3,)),
            pltpu.SemaphoreType.DMA((SEMS,)),
            pltpu.SemaphoreType.DMA((SEMS,)),
        ],
        compiler_params=pltpu.CompilerParams(
            collective_id=0, has_side_effects=True, vmem_limit_bytes=56 * 2**20
        ),
        cost_estimate=pl.CostEstimate(flops=10**9, bytes_accessed=4 * 2**20, transcendentals=2**17),
        name="layer",
    )(features.reshape(4, TB, 256), weight, cotangent, tiles.reshape(NT, TB, TB), idx)
    return act, fg, wg


def solution(mesh):
    return jax.shard_map(
        body,
        mesh=mesh,
        in_specs=(
            P(("col", "row"), None),
            P(),
            P(("row", "col"), None),
            P("row", "col", None, None, None),
            P("row", "col", None, None),
        ),
        out_specs=(P(("row", "col"), None), P(("col", "row"), None), P()),
        check_vma=False,
    )
```

```python
import jax
import jax.numpy as jnp
from jax import lax
from jax.experimental import pallas as pl
from jax.experimental.pallas import tpu as pltpu
from jax.sharding import PartitionSpec as P

MESH = pl.DeviceIdType.MESH
BF = jnp.bfloat16
F32 = jnp.float32
TB = 128
NT = 32
NZ = 8
NX = 4
SLOTS = NT + 1
SIZES = (64, 64)
PLAN_X = ('ab', 'ba')
PLAN_F = ('aa', 'ab')
PLAN_D = ('ba', 'aa')
PLAN_B = ('ab', 'ba')
GATE_X = 2
GATE_D = 2
RANKS = ((0, 0), (0, 0))
SEMS = 320
INF = 1e9


def dot(a, b, da, db):
    return lax.dot_general(a, b, (((da,), (db,)), ((), ())), preferred_element_type=F32)


def wrap(v, n):
    return lax.rem(v + n, n)


class Handle:
    def __init__(self, copy, left, eta):
        self.copy, self.left, self.eta = copy, left, eta
        self.waited = self.sent = False

    def wait(self):
        if not self.waited:
            self.copy.wait_recv()
            self.waited = True

    def wait_send(self):
        if not self.sent:
            self.copy.wait_send()
            self.sent = True


class Count:
    def __init__(self, net, need):
        self.net, self.need, self.eta = net, need, INF

    def hit(self):
        self.need -= 1
        if self.need == 0:
            self.eta = self.net.now

    def wait(self):
        pass


class Later:
    def __init__(self):
        self.handle = None

    @property
    def eta(self):
        return INF if self.handle is None else self.handle.eta

    def wait(self):
        self.handle.wait()


class Net:
    def __init__(self, send, recv):
        self.send, self.recv, self.used, self.started = send, recv, 0, []
        self.now, self.free, self.tasks, self.turn, self.fillers = 0.0, {}, [], 0, []

    def copy(self, src, dst, device, link, size):
        c = pltpu.make_async_remote_copy(
            src_ref=src,
            dst_ref=dst,
            send_sem=self.send.at[self.used],
            recv_sem=self.recv.at[self.used],
            device_id=device,
            device_id_type=MESH,
        )
        self.used += 1
        c.start()
        rate = 400.0 if link == "c" else 43.0
        late = {"c": 1.0, "y2": 2.7, "x2": 2.7, "w": 8.0}.get(link, 1.6)
        names = {"y2": ("y",), "x2": ("x+", "x-")}.get(link, (link,))
        start = max([self.now] + [self.free.get(name, 0.0) for name in names])
        left = start + size / 1000.0 / rate
        for name in names:
            self.free[name] = left
        self.now += 0.08
        handle = Handle(c, left, left + late)
        self.started.append(handle)
        return handle

    def spawn(self, task, rank=0):
        self.turn += 1
        self.tasks.append([task, None, rank, self.turn])

    def run(self):
        while self.tasks:
            best, key = None, None
            for t in self.tasks:
                eta = self.now if t[1] is None else max(t[1].eta, self.now)
                k = (eta, t[2], t[3])
                if key is None or k < key:
                    best, key = t, k
            assert key[0] < INF, "stuck"
            if key[0] - self.now > 0.6 and self.fillers:
                cost, work = self.fillers.pop(0)
                work()
                self.now += cost
                continue
            old = [e for e in self.started if not e.sent and e.left + 4.0 < self.now]
            for e in old[: max(0, int((key[0] - self.now) / 0.04))]:
                e.wait_send()
                self.now += 0.03
            self.now = max(self.now, key[0])
            if best[1] is not None:
                best[1].wait()
            self.turn += 1
            best[3] = self.turn
            try:
                best[1] = next(best[0])
            except StopIteration:
                self.tasks.remove(best)
        for cost, work in self.fillers:
            work()
        self.fillers = []

    def finish(self):
        for e in self.started:
            e.wait_send()


class Ring:
    def __init__(self, net, n, k, p, dev, axis, y, fc):
        self.net, self.n, self.m, self.k, self.p, self.q = net, n, n // 2, k, p, 1 - p
        self.dev, self.axis, self.y, self.fc = dev, axis, y, fc

    def side(self, d):
        return self.dev(wrap(self.k + 1, self.n) if d == 0 else wrap(self.k - 1, self.n), self.p)

    def ring(self, src, dst, d, cnt):
        return self.net.copy(src, dst, self.side(d), self.axis + "+-"[d], cnt * self.fc * TB * 2)

    def place(self, o):
        return (None, "x+", "x2", "x-")[o], self.dev(wrap(self.k + o, self.n), self.p)

    def straight(self, src, dst, o, cnt):
        link, device = self.place(o)
        return self.net.copy(src, dst, device, link, cnt * self.fc * TB * 2)

    def across(self, src, dst, cnt):
        return self.net.copy(src, dst, self.dev(self.k, self.q), self.y, cnt * self.fc * TB * 2)

    def gather(self, plan, own, slot, rank, gate):
        net, m, n, k, p, q = self.net, self.m, self.n, self.k, self.p, self.q
        if plan in "de":
            return self.gather_straight(plan, own, slot, rank)
        first = plan == "a"
        issued = Count(net, 4 if first else 2)
        done = Count(net, 4 if first else 2 * m + 3)

        def origin(d, s):
            return wrap(k - s, n) if d == 0 else wrap(k + s, n)

        def arrive(c):
            yield c
            done.hit()

        def over(o, lo, cnt, src):
            net.spawn(arrive(self.across(src, slot(p, o, lo, cnt), cnt)), rank)

        def chain(pp, d, src, c):
            if c is not None:
                yield c
            for s in range(1, m + 1):
                o = origin(d, s - 1)
                lo, cnt = (0, 4) if s < m else (2 * d, 2)
                here = slot(pp, o, lo, cnt) if s > 1 or src is None else src
                c = self.ring(here, slot(pp, o, lo, cnt), d, cnt)
                if s > 1 and not first:
                    over(o, 0, 4, slot(pp, o, 0, 4))
                if s == gate:
                    issued.hit()
                if s < m:
                    yield c
            yield c
            if not first:
                o = origin(d, m)
                over(o, 2 * d, 2, slot(pp, o, 2 * d, 2))
            done.hit()

        if first:
            ya = self.across(own, slot(p, k, 0, 4), 4)
            for d in (0, 1):
                net.spawn(chain(p, d, own, None), rank)
            for d in (0, 1):
                net.spawn(chain(q, d, None, ya), rank)
        else:
            for d in (0, 1):
                net.spawn(chain(p, d, own, None), rank)

            def start():
                yield None
                over(k, 0, 4, own)

            net.spawn(start(), rank)
        return issued, done

    def gather_straight(self, plan, own, slot, rank):
        net, n, k, p, q = self.net, self.n, self.k, self.p, self.q
        offsets = (2, 1, 3)
        issued = Count(net, 1)
        done = Count(net, 6 if plan == "e" else 4)

        def arrive(c):
            yield c
            done.hit()

        if plan == "e":
            ya = self.across(own, slot(p, k, 0, 4), 4)
            for o in offsets:
                net.spawn(arrive(self.straight(own, slot(p, k, 0, 4), o, 4)), rank)

            def onward():
                yield ya
                for o in offsets:
                    net.spawn(arrive(self.straight(slot(q, k, 0, 4), slot(q, k, 0, 4), o, 4)), rank)
                issued.hit()

            net.spawn(onward(), rank)
        else:
            net.spawn(arrive(self.across(own, slot(p, k, 0, 4), 4)), rank)
            came = {o: self.straight(own, slot(p, k, 0, 4), o, 4) for o in offsets}
            issued.hit()

            def onward(o):
                yield came[o]
                t = slot(p, wrap(k - o, n), 0, 4)
                net.spawn(arrive(self.across(t, t, 4)), rank)

            for o in offsets:
                net.spawn(onward(o), rank)
        return issued, done

    def scatter(self, plan, part, bufs, out, rank):
        net, m, n, k, p, q = self.net, self.m, self.n, self.k, self.p, self.q
        done = Count(net, 1)

        def emit(dst, lo, cnt, terms):
            def one(i, unused):
                total = terms[0](i)
                for t in terms[1:]:
                    total = total + t(i)
                dst[i] = total.astype(BF)
                return unused

            lax.fori_loop(lo, lo + cnt, one, 0)
            net.now += 0.05 * cnt

        def read(ref):
            return lambda i: ref[i].astype(F32)

        def mine(pp, t):
            return lambda i: part(pp, t, i)

        def offset(d, s):
            return m + 1 - s if d == 0 else (n - (m + 1 - s)) % n

        def step(src, dst, d, s, terms, before):
            if s == 1:
                lo = 2 * d
                emit(src, lo, 2, terms)
                return self.ring(src.at[pl.ds(lo, 2)], dst.at[pl.ds(lo, 2)], d, 2)
            if s == 2:
                emit(src, 2 * d, 2, terms + [read(before)])
                emit(src, 2 - 2 * d, 2, terms)
            else:
                emit(src, 0, 4, terms + [read(before)])
            return self.ring(src, dst, d, 4)

        if plan in "de":
            offsets = (2, 1, 3)
        if plan == "e":
            sa, ra, sya, rya = bufs

            def final():
                came = {}
                for j, pp in ((0, q), (1, p)):
                    for o in offsets:
                        emit(sa.at[j, o], 0, 4, [mine(pp, wrap(k + o, n))])
                        came[j, o] = self.straight(sa.at[j, o], ra.at[j, o], o, 4)
                        yield None
                for o in offsets:
                    yield came[0, o]
                emit(sya, 0, 4, [mine(q, k)] + [read(ra.at[0, o]) for o in offsets])
                c = self.across(sya, rya, 4)
                for o in offsets:
                    yield came[1, o]
                yield c
                emit(out, 0, 4, [mine(p, k)] + [read(ra.at[1, o]) for o in offsets] + [read(rya)])
                done.hit()

            net.spawn(final(), rank)
        elif plan == "d":
            sb, rb, sy, ry = bufs

            def final():
                ys, came = {}, {}
                for o in offsets + (0,):
                    emit(sy.at[o], 0, 4, [mine(q, wrap(k + o, n))])
                    ys[o] = self.across(sy.at[o], ry.at[o], 4)
                    yield None
                for o in offsets:
                    yield ys[o]
                    emit(sb.at[o], 0, 4, [mine(p, wrap(k + o, n)), read(ry.at[o])])
                    came[o] = self.straight(sb.at[o], rb.at[o], o, 4)
                yield ys[0]
                for o in offsets:
                    yield came[o]
                emit(out, 0, 4, [mine(p, k), read(ry.at[0])] + [read(rb.at[o]) for o in offsets])
                done.hit()

            net.spawn(final(), rank)
        elif plan == "a":
            sa, ra, sya, rya = bufs
            rings = [Count(net, 2), Count(net, 2)]

            def chain(j, pp, d):
                for s in range(1, m + 1):
                    t = wrap(k + offset(d, s), n)
                    c = step(sa.at[j, d, s - 1], ra.at[j, d, s - 1], d, s, [mine(pp, t)], ra.at[j, d, max(s - 2, 0)])
                    yield c
                rings[j].hit()

            def last(j):
                return [read(ra.at[j, 0, m - 1]), read(ra.at[j, 1, m - 1])]

            def final():
                yield rings[0]
                emit(sya, 0, 4, [mine(q, k)] + last(0))
                c = self.across(sya, rya, 4)
                yield rings[1]
                yield c
                emit(out, 0, 4, [mine(p, k)] + last(1) + [read(rya)])
                done.hit()

            for j, pp in ((0, q), (1, p)):
                for d in (0, 1):
                    net.spawn(chain(j, pp, d), rank)
            net.spawn(final(), rank)
        else:
            sb, rb, sy, ry = bufs
            ys = [Later() for i in range(n)]
            rings = Count(net, 2)

            def send():
                order = [m]
                for s in range(2, m + 1):
                    order += [offset(0, s), offset(1, s)]
                for o in order + [0]:
                    emit(sy.at[o], 0, 4, [mine(q, wrap(k + o, n))])
                    ys[o].handle = self.across(sy.at[o], ry.at[o], 4)
                    yield None

            def chain(d):
                for s in range(1, m + 1):
                    o = offset(d, s)
                    yield ys[o]
                    terms = [mine(p, wrap(k + o, n)), read(ry.at[o])]
                    c = step(sb.at[d, s - 1], rb.at[d, s - 1], d, s, terms, rb.at[d, max(s - 2, 0)])
                    yield c
                rings.hit()

            def final():
                yield rings
                yield ys[0]
                emit(out, 0, 4, [mine(p, k), read(ry.at[0]), read(rb.at[0, m - 1]), read(rb.at[1, m - 1])])
                done.hit()

            net.spawn(send(), rank)
            for d in (0, 1):
                net.spawn(chain(d), rank)
            net.spawn(final(), rank)
        return done


def kernel(
    x_hbm, w_hbm, cot_hbm, tiles_hbm, idx_hbm, act_ref, fg_ref, wg_ref,
    xv, wv, cotv, wt, cott, tiles, idx, xo, xs, gs, sums, aggs, af, dall, ds, dg, fgs, fo,
    fbufs, bbufs, wpart, wpair, wrow, wmine, wcol, wfull,
    local, send, recv,
):
    row, col = lax.axis_index("row"), lax.axis_index("col")
    p, z = lax.div(row, NZ), lax.rem(row, NZ)
    h = lax.rem(col, 2)
    chip = lax.div(col, 2)
    x, u = lax.div(chip, 2), lax.rem(chip, 2)
    other = (row, col + 1 - 2 * h)
    net = Net(send, recv)
    along_z = [Ring(net, NZ, z, p, lambda k, pp: (pp * NZ + k, col), "z", "y", fc) for fc in SIZES]
    along_x = [Ring(net, NX, x, u, lambda k, pp: (row, (k * 2 + pp) * 2 + h), "x", "y2", fc) for fc in SIZES]
    mates = [(wrap(row + d, 16), col) for d in range(1, 16)]
    chips = [(row, wrap(chip + d, 8) * 2 + h) for d in range(1, 8)]
    chunks = range(len(SIZES))
    offsets = [sum(SIZES[:c]) for c in chunks]
    bytes_of = [4 * fc * TB * 2 for fc in SIZES]

    barrier = pltpu.get_barrier_semaphore()
    for device in mates + chips + [other]:
        pl.semaphore_signal(barrier, inc=1, device_id=device, device_id_type=MESH)

    pairs = ((x_hbm, xv), (idx_hbm, idx.at[h]), (tiles_hbm, tiles.at[h]), (w_hbm, wv), (cot_hbm, cotv))
    loads = [pltpu.make_async_copy(a, b, local.at[i]) for i, (a, b) in enumerate(pairs)]
    for c in loads:
        c.start()
    for c in chunks:
        sums[c][0] = jnp.zeros((SIZES[c], TB), F32)
        sums[c][SLOTS] = jnp.zeros((SIZES[c], TB), F32)

    mine = pl.ds(pl.multiple_of(h * TB, TB), TB)
    theirs = pl.ds(pl.multiple_of((1 - h) * TB, TB), TB)
    loads[0].wait()
    for b in range(4):
        block = xv[b, :, theirs].T
        for c in chunks:
            xo[c][b] = block[offsets[c]:offsets[c] + SIZES[c]]
    for b in range(4):
        block = xv[b, :, mine].T
        for c in chunks:
            xs[c][h, b] = block[offsets[c]:offsets[c] + SIZES[c]]
    pl.semaphore_wait(barrier, 23)

    rx = [net.copy(xo[c], xs[c].at[h], other, "c", bytes_of[c]) for c in chunks]
    ri = net.copy(idx_hbm, idx.at[h], other, "c", 4096)
    rt = net.copy(tiles_hbm, tiles.at[h], other, "c", 2**20)

    def g_slot(c, g):
        return lambda pp, k, lo, cnt: gs[c][g].at[pl.ds((pp * NZ + k) * 4 + lo, cnt)]

    def d_slot(c, g):
        return lambda pp, k, lo, cnt: dg[c].at[pl.ds(((k * 2 + pp) * 2 + g) * 4 + lo, cnt)]

    def multiply(c, g, source, at, side):
        def one(t, unused):
            product = dot(source[idx[g, at + 1, t]], tiles[g, idx[g, at, t]], 1, side)
            keep = idx[g, at + 2, t].astype(F32)
            sums[c][g * SLOTS + 1 + t] = product + keep * sums[c][g * SLOTS + t]
            return unused

        lax.fori_loop(0, NT, one, 0, unroll=4)
        net.now += 0.35

    def forward_part(c, g):
        def part(pp, k, i):
            at = ((k * 2 + pp) * 2 + g) * 4 + i
            return sums[c][idx[0, 3, at]] + sums[c][SLOTS + idx[1, 3, at]]

        return part

    def backward_part(c, g):
        return lambda pp, k, i: sums[c][g * SLOTS + idx[g, 7, (pp * NZ + k) * 4 + i]]

    issued_x = [None] * len(SIZES)

    def forward(c):
        if c:
            for e in issued_x[c - 1]:
                yield e
        rx[c].wait()
        events = [along_z[c].gather(PLAN_X[c][g], xs[c].at[g], g_slot(c, g), RANKS[0][0] + c, GATE_X) for g in (0, 1)]
        issued_x[c] = [e[0] for e in events]
        for g in (0, 1):
            gs[c][g][pl.ds(row * 4, 4)] = xs[c][g]
        if c + 1 < len(SIZES):
            net.spawn(forward(c + 1), RANKS[0][0] + c + 1)
        if c == 0:
            for e in loads[1:3]:
                e.wait()
            yield ri
            yield rt
        for g in (0, 1):
            yield events[g][1]
            multiply(c, g, gs[c][g], 0, 1)
        dones = [
            along_x[c].scatter(PLAN_F[c][g], forward_part(c, g), fbufs[c][g], aggs[c].at[g], RANKS[0][1] + c)
            for g in (0, 1)
        ]
        for e in dones:
            yield e
        ra = net.copy(aggs[c].at[1 - h], af[c].at[h], other, "c", bytes_of[c])
        af[c][h] = aggs[c][h]
        yield ra

    def turn_weight():
        loads[3].wait()
        wt[...] = wv[...].T

    def turn_cotangent(i):
        def work():
            if i == 0:
                loads[4].wait()
            here = slice(i * TB, (i + 1) * TB)
            cott[:, here] = cotv[here, :].T

        return work

    net.fillers = [(0.4, turn_weight)] + [(0.4, turn_cotangent(i)) for i in range(4)]
    net.spawn(forward(0))
    net.run()

    agg = jnp.concatenate(
        [jnp.concatenate([af[c][e, b] for b in range(4)], axis=1) for e in (0, 1) for c in chunks], axis=0
    )
    pre = dot(wt[...], agg, 1, 0)
    sigma = jax.nn.sigmoid(pre)
    dpre = (cott[...].astype(F32) * sigma * (1.0 + pre * (1.0 - sigma))).astype(BF)
    dagg = dot(wv[...], dpre, 1, 0).astype(BF)
    for e in (0, 1):
        for c in chunks:
            for b in range(4):
                lo = e * TB + offsets[c]
                dall[c][e, b] = dagg[lo:lo + SIZES[c], b * TB:(b + 1) * TB]
    rd = [net.copy(dall[c].at[1 - h], ds[c].at[h], other, "c", bytes_of[c]) for c in chunks]
    for c in chunks:
        ds[c][h] = dall[c][h]
    act_ref[...] = (pre * sigma).astype(BF)
    issued_d = [None] * len(SIZES)

    def backward(c):
        if c:
            for e in issued_d[c - 1]:
                yield e
        yield rd[c]
        events = [along_x[c].gather(PLAN_D[c][g], ds[c].at[g], d_slot(c, g), RANKS[1][0] + c, GATE_D) for g in (0, 1)]
        issued_d[c] = [e[0] for e in events]
        for g in (0, 1):
            dg[c][pl.ds(chip * 8 + g * 4, 4)] = ds[c][g]
        if c == 0:
            wpart[...] = dot(agg, dpre, 1, 1)
            net.now += 0.5
            net.spawn(weights(), 9)
        if c + 1 < len(SIZES):
            net.spawn(backward(c + 1), RANKS[1][0] + c + 1)
        for g in (0, 1):
            yield events[g][1]
        for g in (0, 1):
            multiply(c, g, dg[c], 4, 0)
        dones = [
            along_z[c].scatter(PLAN_B[c][g], backward_part(c, g), bbufs[c][g], fgs[c].at[g], RANKS[1][1] + c)
            for g in (0, 1)
        ]
        for e in dones:
            yield e
        rf = net.copy(fgs[c].at[1 - h], fo[c].at[h], other, "c", bytes_of[c])
        fo[c][h] = fgs[c][h]
        yield rf
        for e in (0, 1):
            lo = e * TB + offsets[c]
            for b in range(4):
                fg_ref[lo:lo + SIZES[c], b * TB:(b + 1) * TB] = fo[c][e, b]

    def weights():
        half = pl.ds(pl.multiple_of(h * TB, TB), TB)
        yield net.copy(wpart.at[pl.ds(pl.multiple_of((1 - h) * TB, TB), TB)], wpair, other, "c", 2**17)
        wpair[...] = wpair[...] + wpart[half]
        own = wpair[pl.ds(pl.multiple_of(row * 8, 8), 8)]
        wrow[row] = own
        cs = [
            net.copy(wpair.at[pl.ds(pl.multiple_of(d[0] * 8, 8), 8)], wrow.at[row], d, "w", 2**13) for d in mates
        ]
        for c in cs:
            yield c
        total = wrow[0]
        for i in range(1, 16):
            total = total + wrow[i]
        wmine[...] = total
        wcol[chip] = total
        cs = [net.copy(wmine, wcol.at[chip], d, "w", 2**13) for d in chips]
        for c in cs:
            yield c
        total = wcol[0]
        for i in range(1, 8):
            total = total + wcol[i]
        here = pl.ds(pl.multiple_of(h * TB + row * 8, 8), 8)
        wfull[here] = total
        cs = [net.copy(wfull.at[here], wfull.at[here], d, "w", 2**13) for d in mates]
        for c in cs:
            yield c
        yield net.copy(wfull.at[half], wfull.at[half], other, "c", 2**17)
        wg_ref[...] = wfull[...]

    net.spawn(backward(0))
    net.run()
    net.finish()


def order_of(targets, sources):
    key = targets * 64 + sources
    rank = jnp.sum((key[None, :] < key[:, None]).astype(jnp.int32), axis=1)
    place = (rank[None, :] == jnp.arange(NT)[:, None]).astype(jnp.int32)
    before = (rank[None, :] == jnp.arange(NT)[:, None] - 1).astype(jnp.int32)
    perm = jnp.sum(place * jnp.arange(NT)[None, :], axis=1)
    source = jnp.sum(place * sources[None, :], axis=1)
    now = jnp.sum(place * targets[None, :], axis=1)
    last = jnp.sum(before * (targets + 1)[None, :], axis=1) - 1
    same = (now == last).astype(jnp.int32)
    blocks = jnp.arange(64)
    upto = jnp.sum((targets[None, :] <= blocks[:, None]).astype(jnp.int32), axis=1)
    found = jnp.max((targets[None, :] == blocks[:, None]).astype(jnp.int32), axis=1)
    wide = lambda v: jnp.pad(v, (0, 128 - v.shape[0]))
    return [wide(perm), wide(source), wide(same), wide(upto * found)]


def turn(act_t, fg_t, wg_in, act_ref, fg_ref, wg_ref):
    for b in range(4):
        here = slice(b * TB, (b + 1) * TB)
        act_ref[here, :] = act_t[:, here].T
        fg_ref[here, :] = fg_t[:, here].T
    wg_ref[...] = wg_in[...]


def body(features, weight, cotangent, tiles, coords):
    rows, cols = coords[0, 0, 0], coords[0, 0, 1]
    idx = jnp.stack(order_of(rows, cols) + order_of(cols, rows)).astype(jnp.int32)
    vmem = pl.BlockSpec(memory_space=pltpu.VMEM)
    hbm = pl.BlockSpec(memory_space=pl.ANY)

    def units(c, *lead):
        return pltpu.VMEM((*lead, 4, SIZES[c], TB), BF)

    def each(*lead):
        return [units(c, *lead) for c in range(len(SIZES))]

    def sums_for(n, plan):
        m = n // 2
        shapes = {"a": ((2, 2, m), (2, 2, m), (), ()), "b": ((2, m), (2, m), (n,), (n,))}
        shapes |= {"e": ((2, n), (2, n), (), ()), "d": ((n,), (n,), (n,), (n,))}
        return [[[units(c, *t) for t in shapes[kind]] for kind in plan[c]] for c in range(len(SIZES))]

    def blocks():
        return [pltpu.VMEM((64, fc, TB), BF) for fc in SIZES]

    act, fg, wg = pl.pallas_call(
        kernel,
        out_shape=(
            jax.ShapeDtypeStruct((256, 512), BF),
            jax.ShapeDtypeStruct((256, 512), BF),
            jax.ShapeDtypeStruct((256, 256), F32),
        ),
        in_specs=[hbm] * 5,
        out_specs=(vmem, vmem, vmem),
        scratch_shapes=[
            pltpu.VMEM((4, TB, 256), BF),
            pltpu.VMEM((256, 256), BF),
            pltpu.VMEM((512, 256), BF),
            pltpu.VMEM((256, 256), BF),
            pltpu.VMEM((256, 512), BF),
            pltpu.VMEM((2, NT, TB, TB), BF),
            pltpu.SMEM((2, 8, TB), jnp.int32),
            each(),
            each(2),
            [list(pair) for pair in zip(blocks(), blocks())],
            [pltpu.VMEM((2 * SLOTS, fc, TB), F32) for fc in SIZES],
            each(2),
            each(2),
            each(2),
            each(2),
            blocks(),
            each(2),
            each(2),
            sums_for(NX, PLAN_F),
            sums_for(NZ, PLAN_B),
            pltpu.VMEM((256, 256), F32),
            pltpu.VMEM((128, 256), F32),
            pltpu.VMEM((16, 8, 256), F32),
            pltpu.VMEM((8, 256), F32),
            pltpu.VMEM((8, 8, 256), F32),
            pltpu.VMEM((256, 256), F32),
            pltpu.SemaphoreType.DMA((5,)),
            pltpu.SemaphoreType.DMA((SEMS,)),
            pltpu.SemaphoreType.DMA((SEMS,)),
        ],
        compiler_params=pltpu.CompilerParams(
            collective_id=0, has_side_effects=True, vmem_limit_bytes=56 * 2**20
        ),
        cost_estimate=pl.CostEstimate(flops=10**9, bytes_accessed=4 * 2**20, transcendentals=2**17),
        name="layer",
    )(features.reshape(4, TB, 256), weight, cotangent, tiles.reshape(NT, TB, TB), idx)
    return pl.pallas_call(
        turn,
        out_shape=(
            jax.ShapeDtypeStruct((512, 256), BF),
            jax.ShapeDtypeStruct((512, 256), BF),
            jax.ShapeDtypeStruct((256, 256), F32),
        ),
        in_specs=[vmem] * 3,
        out_specs=(vmem, vmem, vmem),
        name="turn",
    )(act, fg, wg)


def solution(mesh):
    return jax.shard_map(
        body,
        mesh=mesh,
        in_specs=(
            P(("col", "row"), None),
            P(),
            P(("row", "col"), None),
            P("row", "col", None, None, None),
            P("row", "col", None, None),
        ),
        out_specs=(P(("row", "col"), None), P(("col", "row"), None), P()),
        check_vma=False,
    )
```

```python
import jax
import jax.numpy as jnp
from jax import lax
from jax.experimental import pallas as pl
from jax.experimental.pallas import tpu as pltpu
from jax.sharding import PartitionSpec as P

MESH = pl.DeviceIdType.MESH
BF = jnp.bfloat16
F32 = jnp.float32
TB = 128
NT = 32
NZ = 8
NX = 4
SLOTS = NT + 1
SIZES = (80, 48)
PLAN_X = ('ab', 'ba')
PLAN_F = ('aa', 'ab')
PLAN_D = ("de","ee")
PLAN_B = ('ba', 'ba')
GATE_X = 2
GATE_D = 2
RANKS = ((0, 0), (0, 0))
SEMS = 320
INF = 1e9


def dot(a, b, da, db):
    return lax.dot_general(a, b, (((da,), (db,)), ((), ())), preferred_element_type=F32)


def wrap(v, n):
    return lax.rem(v + n, n)


class Handle:
    def __init__(self, copy, left, eta):
        self.copy, self.left, self.eta = copy, left, eta
        self.waited = self.sent = False

    def wait(self):
        if not self.waited:
            self.copy.wait_recv()
            self.waited = True

    def wait_send(self):
        if not self.sent:
            self.copy.wait_send()
            self.sent = True


class Count:
    def __init__(self, net, need):
        self.net, self.need, self.eta = net, need, INF

    def hit(self):
        self.need -= 1
        if self.need == 0:
            self.eta = self.net.now

    def wait(self):
        pass


class Later:
    def __init__(self):
        self.handle = None

    @property
    def eta(self):
        return INF if self.handle is None else self.handle.eta

    def wait(self):
        self.handle.wait()


class Net:
    def __init__(self, send, recv):
        self.send, self.recv, self.used, self.started = send, recv, 0, []
        self.now, self.free, self.tasks, self.turn, self.fillers = 0.0, {}, [], 0, []

    def copy(self, src, dst, device, link, size):
        c = pltpu.make_async_remote_copy(
            src_ref=src,
            dst_ref=dst,
            send_sem=self.send.at[self.used],
            recv_sem=self.recv.at[self.used],
            device_id=device,
            device_id_type=MESH,
        )
        self.used += 1
        c.start()
        rate = 400.0 if link == "c" else 43.0
        late = {"c": 1.0, "y2": 2.7, "x2": 2.7, "w": 8.0}.get(link, 1.6)
        names = {"y2": ("y",), "x2": ("x+", "x-")}.get(link, (link,))
        start = max([self.now] + [self.free.get(name, 0.0) for name in names])
        left = start + size / 1000.0 / rate
        for name in names:
            self.free[name] = left
        self.now += 0.08
        handle = Handle(c, left, left + late)
        self.started.append(handle)
        return handle

    def spawn(self, task, rank=0):
        self.turn += 1
        self.tasks.append([task, None, rank, self.turn])

    def run(self):
        while self.tasks:
            best, key = None, None
            for t in self.tasks:
                eta = self.now if t[1] is None else max(t[1].eta, self.now)
                k = (eta, t[2], t[3])
                if key is None or k < key:
                    best, key = t, k
            assert key[0] < INF, "stuck"
            if key[0] - self.now > 0.6 and self.fillers:
                cost, work = self.fillers.pop(0)
                work()
                self.now += cost
                continue
            old = [e for e in self.started if not e.sent and e.left + 4.0 < self.now]
            for e in old[: max(0, int((key[0] - self.now) / 0.04))]:
                e.wait_send()
                self.now += 0.03
            self.now = max(self.now, key[0])
            if best[1] is not None:
                best[1].wait()
            self.turn += 1
            best[3] = self.turn
            try:
                best[1] = next(best[0])
            except StopIteration:
                self.tasks.remove(best)
        for cost, work in self.fillers:
            work()
        self.fillers = []

    def finish(self):
        for e in self.started:
            e.wait_send()


class Ring:
    def __init__(self, net, n, k, p, dev, axis, y, fc):
        self.net, self.n, self.m, self.k, self.p, self.q = net, n, n // 2, k, p, 1 - p
        self.dev, self.axis, self.y, self.fc = dev, axis, y, fc

    def side(self, d):
        return self.dev(wrap(self.k + 1, self.n) if d == 0 else wrap(self.k - 1, self.n), self.p)

    def ring(self, src, dst, d, cnt):
        return self.net.copy(src, dst, self.side(d), self.axis + "+-"[d], cnt * self.fc * TB * 2)

    def place(self, o):
        return (None, "x+", "x2", "x-")[o], self.dev(wrap(self.k + o, self.n), self.p)

    def straight(self, src, dst, o, cnt):
        link, device = self.place(o)
        return self.net.copy(src, dst, device, link, cnt * self.fc * TB * 2)

    def across(self, src, dst, cnt):
        return self.net.copy(src, dst, self.dev(self.k, self.q), self.y, cnt * self.fc * TB * 2)

    def gather(self, plan, own, slot, rank, gate):
        net, m, n, k, p, q = self.net, self.m, self.n, self.k, self.p, self.q
        if plan in "de":
            return self.gather_straight(plan, own, slot, rank)
        first = plan == "a"
        issued = Count(net, 4 if first else 2)
        done = Count(net, 4 if first else 2 * m + 3)

        def origin(d, s):
            return wrap(k - s, n) if d == 0 else wrap(k + s, n)

        def arrive(c):
            yield c
            done.hit()

        def over(o, lo, cnt, src):
            net.spawn(arrive(self.across(src, slot(p, o, lo, cnt), cnt)), rank)

        def chain(pp, d, src, c):
            if c is not None:
                yield c
            for s in range(1, m + 1):
                o = origin(d, s - 1)
                lo, cnt = (0, 4) if s < m else (2 * d, 2)
                here = slot(pp, o, lo, cnt) if s > 1 or src is None else src
                c = self.ring(here, slot(pp, o, lo, cnt), d, cnt)
                if s > 1 and not first:
                    over(o, 0, 4, slot(pp, o, 0, 4))
                if s == gate:
                    issued.hit()
                if s < m:
                    yield c
            yield c
            if not first:
                o = origin(d, m)
                over(o, 2 * d, 2, slot(pp, o, 2 * d, 2))
            done.hit()

        if first:
            ya = self.across(own, slot(p, k, 0, 4), 4)
            for d in (0, 1):
                net.spawn(chain(p, d, own, None), rank)
            for d in (0, 1):
                net.spawn(chain(q, d, None, ya), rank)
        else:
            for d in (0, 1):
                net.spawn(chain(p, d, own, None), rank)

            def start():
                yield None
                over(k, 0, 4, own)

            net.spawn(start(), rank)
        return issued, done

    def gather_straight(self, plan, own, slot, rank):
        net, n, k, p, q = self.net, self.n, self.k, self.p, self.q
        offsets = (2, 1, 3)
        issued = Count(net, 1)
        done = Count(net, 6 if plan == "e" else 4)

        def arrive(c):
            yield c
            done.hit()

        if plan == "e":
            ya = self.across(own, slot(p, k, 0, 4), 4)
            for o in offsets:
                net.spawn(arrive(self.straight(own, slot(p, k, 0, 4), o, 4)), rank)

            def onward():
                yield ya
                for o in offsets:
                    net.spawn(arrive(self.straight(slot(q, k, 0, 4), slot(q, k, 0, 4), o, 4)), rank)
                issued.hit()

            net.spawn(onward(), rank)
        else:
            net.spawn(arrive(self.across(own, slot(p, k, 0, 4), 4)), rank)
            came = {o: self.straight(own, slot(p, k, 0, 4), o, 4) for o in offsets}
            issued.hit()

            def onward(o):
                yield came[o]
                t = slot(p, wrap(k - o, n), 0, 4)
                net.spawn(arrive(self.across(t, t, 4)), rank)

            for o in offsets:
                net.spawn(onward(o), rank)
        return issued, done

    def scatter(self, plan, part, bufs, out, rank):
        net, m, n, k, p, q = self.net, self.m, self.n, self.k, self.p, self.q
        done = Count(net, 1)

        def emit(dst, lo, cnt, terms):
            def one(i, unused):
                total = terms[0](i)
                for t in terms[1:]:
                    total = total + t(i)
                dst[i] = total.astype(BF)
                return unused

            lax.fori_loop(lo, lo + cnt, one, 0, unroll=True)
            net.now += 0.05 * cnt

        def read(ref):
            return lambda i: ref[i].astype(F32)

        def mine(pp, t):
            return lambda i: part(pp, t, i)

        def offset(d, s):
            return m + 1 - s if d == 0 else (n - (m + 1 - s)) % n

        def step(src, dst, d, s, terms, before):
            if s == 1:
                lo = 2 * d
                emit(src, lo, 2, terms)
                return self.ring(src.at[pl.ds(lo, 2)], dst.at[pl.ds(lo, 2)], d, 2)
            if s == 2:
                emit(src, 2 * d, 2, terms + [read(before)])
                emit(src, 2 - 2 * d, 2, terms)
            else:
                emit(src, 0, 4, terms + [read(before)])
            return self.ring(src, dst, d, 4)

        if plan in "de":
            offsets = (2, 1, 3)
        if plan == "e":
            sa, ra, sya, rya = bufs

            def final():
                came = {}
                for j, pp in ((0, q), (1, p)):
                    for o in offsets:
                        emit(sa.at[j, o], 0, 4, [mine(pp, wrap(k + o, n))])
                        came[j, o] = self.straight(sa.at[j, o], ra.at[j, o], o, 4)
                        yield None
                for o in offsets:
                    yield came[0, o]
                emit(sya, 0, 4, [mine(q, k)] + [read(ra.at[0, o]) for o in offsets])
                c = self.across(sya, rya, 4)
                for o in offsets:
                    yield came[1, o]
                yield c
                emit(out, 0, 4, [mine(p, k)] + [read(ra.at[1, o]) for o in offsets] + [read(rya)])
                done.hit()

            net.spawn(final(), rank)
        elif plan == "d":
            sb, rb, sy, ry = bufs

            def final():
                ys, came = {}, {}
                for o in offsets + (0,):
                    emit(sy.at[o], 0, 4, [mine(q, wrap(k + o, n))])
                    ys[o] = self.across(sy.at[o], ry.at[o], 4)
                    yield None
                for o in offsets:
                    yield ys[o]
                    emit(sb.at[o], 0, 4, [mine(p, wrap(k + o, n)), read(ry.at[o])])
                    came[o] = self.straight(sb.at[o], rb.at[o], o, 4)
                yield ys[0]
                for o in offsets:
                    yield came[o]
                emit(out, 0, 4, [mine(p, k), read(ry.at[0])] + [read(rb.at[o]) for o in offsets])
                done.hit()

            net.spawn(final(), rank)
        elif plan == "a":
            sa, ra, sya, rya = bufs
            rings = [Count(net, 2), Count(net, 2)]

            def chain(j, pp, d):
                for s in range(1, m + 1):
                    t = wrap(k + offset(d, s), n)
                    c = step(sa.at[j, d, s - 1], ra.at[j, d, s - 1], d, s, [mine(pp, t)], ra.at[j, d, max(s - 2, 0)])
                    yield c
                rings[j].hit()

            def last(j):
                return [read(ra.at[j, 0, m - 1]), read(ra.at[j, 1, m - 1])]

            def final():
                yield rings[0]
                emit(sya, 0, 4, [mine(q, k)] + last(0))
                c = self.across(sya, rya, 4)
                yield rings[1]
                yield c
                emit(out, 0, 4, [mine(p, k)] + last(1) + [read(rya)])
                done.hit()

            for j, pp in ((0, q), (1, p)):
                for d in (0, 1):
                    net.spawn(chain(j, pp, d), rank)
            net.spawn(final(), rank)
        else:
            sb, rb, sy, ry = bufs
            ys = [Later() for i in range(n)]
            rings = Count(net, 2)

            def send():
                order = [m]
                for s in range(2, m + 1):
                    order += [offset(0, s), offset(1, s)]
                for o in order + [0]:
                    emit(sy.at[o], 0, 4, [mine(q, wrap(k + o, n))])
                    ys[o].handle = self.across(sy.at[o], ry.at[o], 4)
                    yield None

            def chain(d):
                for s in range(1, m + 1):
                    o = offset(d, s)
                    yield ys[o]
                    terms = [mine(p, wrap(k + o, n)), read(ry.at[o])]
                    c = step(sb.at[d, s - 1], rb.at[d, s - 1], d, s, terms, rb.at[d, max(s - 2, 0)])
                    yield c
                rings.hit()

            def final():
                yield rings
                yield ys[0]
                emit(out, 0, 4, [mine(p, k), read(ry.at[0]), read(rb.at[0, m - 1]), read(rb.at[1, m - 1])])
                done.hit()

            net.spawn(send(), rank)
            for d in (0, 1):
                net.spawn(chain(d), rank)
            net.spawn(final(), rank)
        return done


def kernel(
    x_hbm, w_hbm, cot_hbm, tiles_hbm, idx_hbm, act_ref, fg_ref, wg_ref,
    xv, wv, cotv, wt, cott, tiles, idx, xo, xs, gs, sums, aggs, af, dall, ds, dg, fgs, fo,
    fbufs, bbufs, wpart, wpair, wrow, wmine, wcol, wfull,
    local, send, recv,
):
    row, col = lax.axis_index("row"), lax.axis_index("col")
    p, z = lax.div(row, NZ), lax.rem(row, NZ)
    h = lax.rem(col, 2)
    chip = lax.div(col, 2)
    x, u = lax.div(chip, 2), lax.rem(chip, 2)
    other = (row, col + 1 - 2 * h)
    net = Net(send, recv)
    along_z = [Ring(net, NZ, z, p, lambda k, pp: (pp * NZ + k, col), "z", "y", fc) for fc in SIZES]
    along_x = [Ring(net, NX, x, u, lambda k, pp: (row, (k * 2 + pp) * 2 + h), "x", "y2", fc) for fc in SIZES]
    mates = [(wrap(row + d, 16), col) for d in range(1, 16)]
    chips = [(row, wrap(chip + d, 8) * 2 + h) for d in range(1, 8)]
    chunks = range(len(SIZES))
    offsets = [sum(SIZES[:c]) for c in chunks]
    bytes_of = [4 * fc * TB * 2 for fc in SIZES]

    barrier = pltpu.get_barrier_semaphore()
    for device in mates + chips + [other]:
        pl.semaphore_signal(barrier, inc=1, device_id=device, device_id_type=MESH)

    pairs = ((x_hbm, xv), (idx_hbm, idx.at[0]), (tiles_hbm, tiles.at[0]), (w_hbm, wv), (cot_hbm, cotv))
    loads = [pltpu.make_async_copy(a, b, local.at[i]) for i, (a, b) in enumerate(pairs)]
    for c in loads:
        c.start()
    for c in chunks:
        sums[c][0] = jnp.zeros((SIZES[c], TB), F32)
        sums[c][SLOTS] = jnp.zeros((SIZES[c], TB), F32)

    mine = pl.ds(pl.multiple_of(h * TB, TB), TB)
    theirs = pl.ds(pl.multiple_of((1 - h) * TB, TB), TB)
    loads[0].wait()
    for b in range(4):
        block = xv[b, :, theirs].T
        for c in chunks:
            xo[c][b] = block[offsets[c]:offsets[c] + SIZES[c]]
    for b in range(4):
        block = xv[b, :, mine].T
        for c in chunks:
            xs[c][0, b] = block[offsets[c]:offsets[c] + SIZES[c]]
    pl.semaphore_wait(barrier, 23)

    rx = [net.copy(xo[c], xs[c].at[1], other, "c", bytes_of[c]) for c in chunks]
    ri = net.copy(idx_hbm, idx.at[1], other, "c", 4096)
    rt = net.copy(tiles_hbm, tiles.at[1], other, "c", 2**20)

    def g_slot(c, g):
        return lambda pp, k, lo, cnt: gs[c][g].at[pl.ds((pp * NZ + k) * 4 + lo, cnt)]

    group = (h, 1 - h)

    def d_slot(c, g):
        return lambda pp, k, lo, cnt: dg[c].at[pl.ds(((k * 2 + pp) * 2 + group[g]) * 4 + lo, cnt)]

    def multiply(c, g, source, at, side):
        def one(t, unused):
            product = dot(source[idx[g, at + 1, t]], tiles[g, idx[g, at, t]], 1, side)
            keep = idx[g, at + 2, t].astype(F32)
            sums[c][g * SLOTS + 1 + t] = product + keep * sums[c][g * SLOTS + t]
            return unused

        lax.fori_loop(0, NT, one, 0, unroll=4)
        net.now += 0.35

    def forward_part(c, g):
        def part(pp, k, i):
            at = ((k * 2 + pp) * 2 + group[g]) * 4 + i
            return sums[c][idx[0, 3, at]] + sums[c][SLOTS + idx[1, 3, at]]

        return part

    def backward_part(c, g):
        return lambda pp, k, i: sums[c][g * SLOTS + idx[g, 7, (pp * NZ + k) * 4 + i]]

    issued_x = [None] * len(SIZES)

    def forward(c):
        if c:
            for e in issued_x[c - 1]:
                yield e
        events = []
        for g in (0, 1):
            if g == 1:
                yield rx[c]
            events.append(along_z[c].gather(PLAN_X[c][g], xs[c].at[g], g_slot(c, g), RANKS[0][0] + c, GATE_X))
            gs[c][g][pl.ds(row * 4, 4)] = xs[c][g]
        issued_x[c] = [e[0] for e in events]
        if c + 1 < len(SIZES):
            net.spawn(forward(c + 1), RANKS[0][0] + c + 1)
        if c == 0:
            for e in loads[1:3]:
                e.wait()
            yield ri
            yield rt
        for g in (0, 1):
            yield events[g][1]
            multiply(c, g, gs[c][g], 0, 1)
        dones = [
            along_x[c].scatter(PLAN_F[c][g], forward_part(c, g), fbufs[c][g], aggs[c].at[g], RANKS[0][1] + c - 0.5 * g)
            for g in (1, 0)
        ]
        yield dones[0]
        ra = net.copy(aggs[c].at[1], af[c].at[h], other, "c", bytes_of[c])
        yield dones[1]
        af[c][h] = aggs[c][0]
        yield ra

    def turn_weight():
        loads[3].wait()
        wt[...] = wv[...].T

    def turn_cotangent(i):
        def work():
            if i == 0:
                loads[4].wait()
            here = slice(i * TB, (i + 1) * TB)
            cott[:, here] = cotv[here, :].T

        return work

    net.fillers = [(0.4, turn_weight)] + [(0.4, turn_cotangent(i)) for i in range(4)]
    net.spawn(forward(0))
    net.run()

    agg = jnp.concatenate(
        [jnp.concatenate([af[c][e, b] for b in range(4)], axis=1) for e in (0, 1) for c in chunks], axis=0
    )
    pre = dot(wt[...], agg, 1, 0)
    sigma = jax.nn.sigmoid(pre)
    dpre = (cott[...].astype(F32) * sigma * (1.0 + pre * (1.0 - sigma))).astype(BF)
    dagg = dot(wv[...], dpre, 1, 0).astype(BF)
    for e in (0, 1):
        for c in chunks:
            for b in range(4):
                lo = e * TB + offsets[c]
                dall[c][e, b] = dagg[lo:lo + SIZES[c], b * TB:(b + 1) * TB]
    rd = [net.copy(dall[c].at[1 - h], ds[c].at[1], other, "c", bytes_of[c]) for c in chunks]
    for c in chunks:
        ds[c][0] = dall[c][h]
    act_ref[...] = (pre * sigma).astype(BF)
    issued_d = [None] * len(SIZES)

    def backward(c):
        if c:
            for e in issued_d[c - 1]:
                yield e
        events = []
        for g in (0, 1):
            if g == 1:
                yield rd[c]
            events.append(along_x[c].gather(PLAN_D[c][g], ds[c].at[g], d_slot(c, g), RANKS[1][0] + c, GATE_D))
            dg[c][pl.ds(chip * 8 + group[g] * 4, 4)] = ds[c][g]
        issued_d[c] = [e[0] for e in events]
        if c == 0:
            wpart[...] = dot(agg, dpre, 1, 1)
            net.now += 0.5
            net.spawn(weights(), 9)
        if c + 1 < len(SIZES):
            net.spawn(backward(c + 1), RANKS[1][0] + c + 1)
        for g in (0, 1):
            yield events[g][1]
        for g in (0, 1):
            multiply(c, g, dg[c], 4, 0)
        dones = [
            along_z[c].scatter(PLAN_B[c][g], backward_part(c, g), bbufs[c][g], fgs[c].at[g], RANKS[1][1] + c - 0.5 * g)
            for g in (1, 0)
        ]
        yield dones[0]
        rf = net.copy(fgs[c].at[1], fo[c].at[h], other, "c", bytes_of[c])
        yield dones[1]
        fo[c][h] = fgs[c][0]
        yield rf
        for e in (0, 1):
            lo = e * TB + offsets[c]
            for b in range(4):
                fg_ref[lo:lo + SIZES[c], b * TB:(b + 1) * TB] = fo[c][e, b]

    def weights():
        half = pl.ds(pl.multiple_of(h * TB, TB), TB)
        yield net.copy(wpart.at[pl.ds(pl.multiple_of((1 - h) * TB, TB), TB)], wpair, other, "c", 2**17)
        wpair[...] = wpair[...] + wpart[half]
        own = wpair[pl.ds(pl.multiple_of(row * 8, 8), 8)]
        wrow[row] = own
        cs = [
            net.copy(wpair.at[pl.ds(pl.multiple_of(d[0] * 8, 8), 8)], wrow.at[row], d, "w", 2**13) for d in mates
        ]
        for c in cs:
            yield c
        total = wrow[0]
        for i in range(1, 16):
            total = total + wrow[i]
        wmine[...] = total
        wcol[chip] = total
        cs = [net.copy(wmine, wcol.at[chip], d, "w", 2**13) for d in chips]
        for c in cs:
            yield c
        total = wcol[0]
        for i in range(1, 8):
            total = total + wcol[i]
        here = pl.ds(pl.multiple_of(h * TB + row * 8, 8), 8)
        wfull[here] = total
        cs = [net.copy(wfull.at[here], wfull.at[here], d, "w", 2**13) for d in mates]
        for c in cs:
            yield c
        yield net.copy(wfull.at[half], wfull.at[half], other, "c", 2**17)
        wg_ref[...] = wfull[...]

    net.spawn(backward(0))
    net.run()
    net.finish()


def write_order(coords_ref, order):
    i32 = jnp.int32
    lane = lax.broadcasted_iota(i32, (NT, TB), 1)
    down = lax.broadcasted_iota(i32, (NT, TB), 0)
    small = lax.broadcasted_iota(i32, (NT, NT), 1)
    pick = small == lax.broadcasted_iota(i32, (NT, NT), 0)

    def down_of(values):
        return jnp.sum(jnp.where(pick, values, 0), axis=1, keepdims=True)

    def along(chosen, values):
        return jnp.sum(jnp.where(chosen, values, 0), axis=0, keepdims=True)

    lanes = [jnp.broadcast_to(coords_ref[0, 0, i:i + 1, :], (NT, NT)) for i in (0, 1)]
    downs = [down_of(v) for v in lanes]
    for at, (a, b) in ((0, (0, 1)), (4, (1, 0))):
        key = lanes[a] * 64 + lanes[b]
        target, source = downs[a], downs[b]
        before = key < target * 64 + source
        rank = jnp.sum(jnp.where(before, 1, 0), axis=1, keepdims=True)
        placed = rank == lane
        now = along(placed, target)
        last = along(rank == lane - 1, target + 1) - 1
        order[at:at + 1, :] = along(placed, down)
        order[at + 1:at + 2, :] = along(placed, source)
        order[at + 2:at + 3, :] = jnp.where(now == last, 1, 0)
        upto = along(target <= lane, jnp.ones((NT, TB), i32))
        found = along(target == lane, jnp.ones((NT, TB), i32))
        order[at + 3:at + 4, :] = jnp.where(found > 0, upto, 0)


def turn(act_t, fg_t, wg_in, act_ref, fg_ref, wg_ref):
    for b in range(4):
        here = slice(b * TB, (b + 1) * TB)
        act_ref[here, :] = act_t[:, here].T
        fg_ref[here, :] = fg_t[:, here].T
    wg_ref[...] = wg_in[...]


def body(features, weight, cotangent, tiles, coords):
    vmem = pl.BlockSpec(memory_space=pltpu.VMEM)
    hbm = pl.BlockSpec(memory_space=pl.ANY)
    idx = pl.pallas_call(
        write_order,
        out_shape=jax.ShapeDtypeStruct((8, TB), jnp.int32),
        in_specs=[vmem],
        out_specs=vmem,
        name="order",
    )(coords)

    def units(c, *lead):
        return pltpu.VMEM((*lead, 4, SIZES[c], TB), BF)

    def each(*lead):
        return [units(c, *lead) for c in range(len(SIZES))]

    def sums_for(n, plan):
        m = n // 2
        shapes = {"a": ((2, 2, m), (2, 2, m), (), ()), "b": ((2, m), (2, m), (n,), (n,))}
        shapes |= {"e": ((2, n), (2, n), (), ()), "d": ((n,), (n,), (n,), (n,))}
        return [[[units(c, *t) for t in shapes[kind]] for kind in plan[c]] for c in range(len(SIZES))]

    def blocks():
        return [pltpu.VMEM((64, fc, TB), BF) for fc in SIZES]

    act, fg, wg = pl.pallas_call(
        kernel,
        out_shape=(
            jax.ShapeDtypeStruct((256, 512), BF),
            jax.ShapeDtypeStruct((256, 512), BF),
            jax.ShapeDtypeStruct((256, 256), F32),
        ),
        in_specs=[hbm] * 5,
        out_specs=(vmem, vmem, vmem),
        scratch_shapes=[
            pltpu.VMEM((4, TB, 256), BF),
            pltpu.VMEM((256, 256), BF),
            pltpu.VMEM((512, 256), BF),
            pltpu.VMEM((256, 256), BF),
            pltpu.VMEM((256, 512), BF),
            pltpu.VMEM((2, NT, TB, TB), BF),
            pltpu.SMEM((2, 8, TB), jnp.int32),
            each(),
            each(2),
            [list(pair) for pair in zip(blocks(), blocks())],
            [pltpu.VMEM((2 * SLOTS, fc, TB), F32) for fc in SIZES],
            each(2),
            each(2),
            each(2),
            each(2),
            blocks(),
            each(2),
            each(2),
            sums_for(NX, PLAN_F),
            sums_for(NZ, PLAN_B),
            pltpu.VMEM((256, 256), F32),
            pltpu.VMEM((128, 256), F32),
            pltpu.VMEM((16, 8, 256), F32),
            pltpu.VMEM((8, 256), F32),
            pltpu.VMEM((8, 8, 256), F32),
            pltpu.VMEM((256, 256), F32),
            pltpu.SemaphoreType.DMA((5,)),
            pltpu.SemaphoreType.DMA((SEMS,)),
            pltpu.SemaphoreType.DMA((SEMS,)),
        ],
        compiler_params=pltpu.CompilerParams(
            collective_id=0, has_side_effects=True, vmem_limit_bytes=56 * 2**20
        ),
        cost_estimate=pl.CostEstimate(flops=10**9, bytes_accessed=4 * 2**20, transcendentals=2**17),
        name="layer",
    )(features.reshape(4, TB, 256), weight, cotangent, tiles.reshape(NT, TB, TB), idx)
    return pl.pallas_call(
        turn,
        out_shape=(
            jax.ShapeDtypeStruct((512, 256), BF),
            jax.ShapeDtypeStruct((512, 256), BF),
            jax.ShapeDtypeStruct((256, 256), F32),
        ),
        in_specs=[vmem] * 3,
        out_specs=(vmem, vmem, vmem),
        name="turn",
    )(act, fg, wg)


def solution(mesh):
    return jax.shard_map(
        body,
        mesh=mesh,
        in_specs=(
            P(("col", "row"), None),
            P(),
            P(("row", "col"), None),
            P("row", "col", None, None, None),
            P("row", "col", None, None),
        ),
        out_specs=(P(("row", "col"), None), P(("col", "row"), None), P()),
        check_vma=False,
    )
```

```python
import jax
import jax.numpy as jnp
from jax import lax
from jax.experimental import pallas as pl
from jax.experimental.pallas import tpu as pltpu
from jax.sharding import PartitionSpec as P

MESH = pl.DeviceIdType.MESH
BF = jnp.bfloat16
F32 = jnp.float32
TB = 128
NT = 32
NZ = 8
NX = 4
SLOTS = NT + 1
SIZES = (80, 48)
PLAN_X = ('ab', 'ba')
PLAN_F = ('aa', 'ab')
PLAN_D = ("de","ee")
PLAN_B = ('ba', 'ba')
GATE_X = 2
GATE_D = 1
RANKS = ((0, 0), (0, 0))
SEMS = 320
INF = 1e9
LATE = {"c": 1.5, "y2": 2.7, "x2": 2.7, "w": 8.0, "z": 1.6}
RATE = 43.0
EMIT = 0.05
ISSUE = 0.08
MULTIPLY = 0.7


def dot(a, b, da, db):
    return lax.dot_general(a, b, (((da,), (db,)), ((), ())), preferred_element_type=F32)


def wrap(v, n):
    return lax.rem(v + n, n)


class Handle:
    def __init__(self, copy, left, eta):
        self.copy, self.left, self.eta = copy, left, eta
        self.waited = self.sent = False

    def wait(self):
        if not self.waited:
            self.copy.wait_recv()
            self.waited = True

    def wait_send(self):
        if not self.sent:
            self.copy.wait_send()
            self.sent = True


class Count:
    def __init__(self, net, need):
        self.net, self.need, self.eta = net, need, INF

    def hit(self):
        self.need -= 1
        if self.need == 0:
            self.eta = self.net.now

    def wait(self):
        pass


class Later:
    def __init__(self):
        self.handle = None

    @property
    def eta(self):
        return INF if self.handle is None else self.handle.eta

    def wait(self):
        self.handle.wait()


class Net:
    def __init__(self, send, recv):
        self.send, self.recv, self.used, self.started = send, recv, 0, []
        self.now, self.free, self.tasks, self.turn, self.fillers = 0.0, {}, [], 0, []

    def copy(self, src, dst, device, link, size):
        c = pltpu.make_async_remote_copy(
            src_ref=src,
            dst_ref=dst,
            send_sem=self.send.at[self.used],
            recv_sem=self.recv.at[self.used],
            device_id=device,
            device_id_type=MESH,
        )
        self.used += 1
        c.start()
        rate = 400.0 if link == "c" else RATE
        late = LATE.get(link, LATE["z"])
        names = {"y2": ("y",), "x2": ("x+", "x-")}.get(link, (link,))
        start = max([self.now] + [self.free.get(name, 0.0) for name in names])
        left = start + size / 1000.0 / rate
        for name in names:
            self.free[name] = left
        self.now += ISSUE
        handle = Handle(c, left, left + late)
        self.started.append(handle)
        return handle

    def spawn(self, task, rank=0):
        self.turn += 1
        self.tasks.append([task, None, rank, self.turn])

    def run(self):
        while self.tasks:
            best, key = None, None
            for t in self.tasks:
                eta = self.now if t[1] is None else max(t[1].eta, self.now)
                k = (eta, t[2], t[3])
                if key is None or k < key:
                    best, key = t, k
            assert key[0] < INF, "stuck"
            if key[0] - self.now > 0.6 and self.fillers:
                cost, work = self.fillers.pop(0)
                work()
                self.now += cost
                continue
            old = [e for e in self.started if not e.sent and e.left + 4.0 < self.now]
            for e in old[: max(0, int((key[0] - self.now) / 0.04))]:
                e.wait_send()
                self.now += 0.03
            self.now = max(self.now, key[0])
            if best[1] is not None:
                best[1].wait()
            self.turn += 1
            best[3] = self.turn
            try:
                best[1] = next(best[0])
            except StopIteration:
                self.tasks.remove(best)
        for cost, work in self.fillers:
            work()
        self.fillers = []

    def finish(self):
        for e in self.started:
            e.wait_send()


class Ring:
    def __init__(self, net, n, k, p, dev, axis, y, fc):
        self.net, self.n, self.m, self.k, self.p, self.q = net, n, n // 2, k, p, 1 - p
        self.dev, self.axis, self.y, self.fc = dev, axis, y, fc

    def side(self, d):
        return self.dev(wrap(self.k + 1, self.n) if d == 0 else wrap(self.k - 1, self.n), self.p)

    def ring(self, src, dst, d, cnt):
        return self.net.copy(src, dst, self.side(d), self.axis + "+-"[d], cnt * self.fc * TB * 2)

    def place(self, o):
        return (None, "x+", "x2", "x-")[o], self.dev(wrap(self.k + o, self.n), self.p)

    def straight(self, src, dst, o, cnt):
        link, device = self.place(o)
        return self.net.copy(src, dst, device, link, cnt * self.fc * TB * 2)

    def across(self, src, dst, cnt):
        return self.net.copy(src, dst, self.dev(self.k, self.q), self.y, cnt * self.fc * TB * 2)

    def gather(self, plan, own, slot, rank, gate):
        net, m, n, k, p, q = self.net, self.m, self.n, self.k, self.p, self.q
        if plan in "de":
            return self.gather_straight(plan, own, slot, rank)
        first = plan == "a"
        issued = Count(net, 4 if first else 2)
        done = Count(net, 4 if first else 2 * m + 3)

        def origin(d, s):
            return wrap(k - s, n) if d == 0 else wrap(k + s, n)

        def arrive(c):
            yield c
            done.hit()

        def over(o, lo, cnt, src):
            net.spawn(arrive(self.across(src, slot(p, o, lo, cnt), cnt)), rank)

        def chain(pp, d, src, c):
            if c is not None:
                yield c
            for s in range(1, m + 1):
                o = origin(d, s - 1)
                lo, cnt = (0, 4) if s < m else (2 * d, 2)
                here = slot(pp, o, lo, cnt) if s > 1 or src is None else src
                c = self.ring(here, slot(pp, o, lo, cnt), d, cnt)
                if s > 1 and not first:
                    over(o, 0, 4, slot(pp, o, 0, 4))
                if s == gate:
                    issued.hit()
                if s < m:
                    yield c
            yield c
            if not first:
                o = origin(d, m)
                over(o, 2 * d, 2, slot(pp, o, 2 * d, 2))
            done.hit()

        if first:
            ya = self.across(own, slot(p, k, 0, 4), 4)
            for d in (0, 1):
                net.spawn(chain(p, d, own, None), rank)
            for d in (0, 1):
                net.spawn(chain(q, d, None, ya), rank)
        else:
            for d in (0, 1):
                net.spawn(chain(p, d, own, None), rank)

            def start():
                yield None
                over(k, 0, 4, own)

            net.spawn(start(), rank)
        return issued, done

    def gather_straight(self, plan, own, slot, rank):
        net, n, k, p, q = self.net, self.n, self.k, self.p, self.q
        offsets = (2, 1, 3)
        issued = Count(net, 1)
        done = Count(net, 6 if plan == "e" else 4)

        def arrive(c):
            yield c
            done.hit()

        if plan == "e":
            ya = self.across(own, slot(p, k, 0, 4), 4)
            for o in offsets:
                net.spawn(arrive(self.straight(own, slot(p, k, 0, 4), o, 4)), rank)

            def onward():
                yield ya
                for o in offsets:
                    net.spawn(arrive(self.straight(slot(q, k, 0, 4), slot(q, k, 0, 4), o, 4)), rank)
                issued.hit()

            net.spawn(onward(), rank)
        else:
            net.spawn(arrive(self.across(own, slot(p, k, 0, 4), 4)), rank)
            came = {o: self.straight(own, slot(p, k, 0, 4), o, 4) for o in offsets}
            issued.hit()

            def onward(o):
                yield came[o]
                t = slot(p, wrap(k - o, n), 0, 4)
                net.spawn(arrive(self.across(t, t, 4)), rank)

            for o in offsets:
                net.spawn(onward(o), rank)
        return issued, done

    def scatter(self, plan, part, bufs, out, rank):
        net, m, n, k, p, q = self.net, self.m, self.n, self.k, self.p, self.q
        done = Count(net, 1)

        def emit(dst, lo, cnt, terms):
            def one(i, unused):
                total = terms[0](i)
                for t in terms[1:]:
                    total = total + t(i)
                dst[i] = total.astype(BF)
                return unused

            lax.fori_loop(lo, lo + cnt, one, 0, unroll=True)
            net.now += EMIT * cnt

        def read(ref):
            return lambda i: ref[i].astype(F32)

        def mine(pp, t):
            return lambda i: part(pp, t, i)

        def offset(d, s):
            return m + 1 - s if d == 0 else (n - (m + 1 - s)) % n

        def step(src, dst, d, s, terms, before):
            if s == 1:
                lo = 2 * d
                emit(src, lo, 2, terms)
                return self.ring(src.at[pl.ds(lo, 2)], dst.at[pl.ds(lo, 2)], d, 2)
            if s == 2:
                emit(src, 2 * d, 2, terms + [read(before)])
                emit(src, 2 - 2 * d, 2, terms)
            else:
                emit(src, 0, 4, terms + [read(before)])
            return self.ring(src, dst, d, 4)

        if plan in "de":
            offsets = (2, 1, 3)
        if plan == "e":
            sa, ra, sya, rya = bufs

            def final():
                came = {}
                for j, pp in ((0, q), (1, p)):
                    for o in offsets:
                        emit(sa.at[j, o], 0, 4, [mine(pp, wrap(k + o, n))])
                        came[j, o] = self.straight(sa.at[j, o], ra.at[j, o], o, 4)
                        yield None
                for o in offsets:
                    yield came[0, o]
                emit(sya, 0, 4, [mine(q, k)] + [read(ra.at[0, o]) for o in offsets])
                c = self.across(sya, rya, 4)
                for o in offsets:
                    yield came[1, o]
                yield c
                emit(out, 0, 4, [mine(p, k)] + [read(ra.at[1, o]) for o in offsets] + [read(rya)])
                done.hit()

            net.spawn(final(), rank)
        elif plan == "d":
            sb, rb, sy, ry = bufs

            def final():
                ys, came = {}, {}
                for o in offsets + (0,):
                    emit(sy.at[o], 0, 4, [mine(q, wrap(k + o, n))])
                    ys[o] = self.across(sy.at[o], ry.at[o], 4)
                    yield None
                for o in offsets:
                    yield ys[o]
                    emit(sb.at[o], 0, 4, [mine(p, wrap(k + o, n)), read(ry.at[o])])
                    came[o] = self.straight(sb.at[o], rb.at[o], o, 4)
                yield ys[0]
                for o in offsets:
                    yield came[o]
                emit(out, 0, 4, [mine(p, k), read(ry.at[0])] + [read(rb.at[o]) for o in offsets])
                done.hit()

            net.spawn(final(), rank)
        elif plan == "a":
            sa, ra, sya, rya = bufs
            rings = [Count(net, 2), Count(net, 2)]

            def chain(j, pp, d):
                for s in range(1, m + 1):
                    t = wrap(k + offset(d, s), n)
                    c = step(sa.at[j, d, s - 1], ra.at[j, d, s - 1], d, s, [mine(pp, t)], ra.at[j, d, max(s - 2, 0)])
                    yield c
                rings[j].hit()

            def last(j):
                return [read(ra.at[j, 0, m - 1]), read(ra.at[j, 1, m - 1])]

            def final():
                yield rings[0]
                emit(sya, 0, 4, [mine(q, k)] + last(0))
                c = self.across(sya, rya, 4)
                yield rings[1]
                yield c
                emit(out, 0, 4, [mine(p, k)] + last(1) + [read(rya)])
                done.hit()

            for j, pp in ((0, q), (1, p)):
                for d in (0, 1):
                    net.spawn(chain(j, pp, d), rank)
            net.spawn(final(), rank)
        else:
            sb, rb, sy, ry = bufs
            ys = [Later() for i in range(n)]
            rings = Count(net, 2)

            def send():
                order = [m]
                for s in range(2, m + 1):
                    order += [offset(0, s), offset(1, s)]
                for o in order + [0]:
                    emit(sy.at[o], 0, 4, [mine(q, wrap(k + o, n))])
                    ys[o].handle = self.across(sy.at[o], ry.at[o], 4)
                    yield None

            def chain(d):
                for s in range(1, m + 1):
                    o = offset(d, s)
                    yield ys[o]
                    terms = [mine(p, wrap(k + o, n)), read(ry.at[o])]
                    c = step(sb.at[d, s - 1], rb.at[d, s - 1], d, s, terms, rb.at[d, max(s - 2, 0)])
                    yield c
                rings.hit()

            def final():
                yield rings
                yield ys[0]
                emit(out, 0, 4, [mine(p, k), read(ry.at[0]), read(rb.at[0, m - 1]), read(rb.at[1, m - 1])])
                done.hit()

            net.spawn(send(), rank)
            for d in (0, 1):
                net.spawn(chain(d), rank)
            net.spawn(final(), rank)
        return done


def kernel(
    x_hbm, w_hbm, cot_hbm, tiles_hbm, idx_hbm, act_ref, fg_ref, wg_ref,
    xv, wv, cotv, wt, cott, tiles, idx, xo, xs, gs, sums, aggs, af, dall, ds, dg, fgs, fo,
    fbufs, bbufs, wpart, wpair, wrow, wmine, wcol, wfull,
    local, send, recv,
):
    row, col = lax.axis_index("row"), lax.axis_index("col")
    p, z = lax.div(row, NZ), lax.rem(row, NZ)
    h = lax.rem(col, 2)
    chip = lax.div(col, 2)
    x, u = lax.div(chip, 2), lax.rem(chip, 2)
    other = (row, col + 1 - 2 * h)
    net = Net(send, recv)
    along_z = [Ring(net, NZ, z, p, lambda k, pp: (pp * NZ + k, col), "z", "y", fc) for fc in SIZES]
    along_x = [Ring(net, NX, x, u, lambda k, pp: (row, (k * 2 + pp) * 2 + h), "x", "y2", fc) for fc in SIZES]
    mates = [(wrap(row + d, 16), col) for d in range(1, 16)]
    chips = [(row, wrap(chip + d, 8) * 2 + h) for d in range(1, 8)]
    chunks = range(len(SIZES))
    offsets = [sum(SIZES[:c]) for c in chunks]
    bytes_of = [4 * fc * TB * 2 for fc in SIZES]

    barrier = pltpu.get_barrier_semaphore()
    for device in mates + chips + [other]:
        pl.semaphore_signal(barrier, inc=1, device_id=device, device_id_type=MESH)

    pairs = ((x_hbm, xv), (idx_hbm, idx.at[0]), (tiles_hbm, tiles.at[0]), (w_hbm, wv), (cot_hbm, cotv))
    loads = [pltpu.make_async_copy(a, b, local.at[i]) for i, (a, b) in enumerate(pairs)]
    for c in loads:
        c.start()
    for c in chunks:
        sums[c][0] = jnp.zeros((SIZES[c], TB), F32)
        sums[c][SLOTS] = jnp.zeros((SIZES[c], TB), F32)

    mine = pl.ds(pl.multiple_of(h * TB, TB), TB)
    theirs = pl.ds(pl.multiple_of((1 - h) * TB, TB), TB)
    loads[0].wait()
    for b in range(4):
        block = xv[b, :, theirs].T
        for c in chunks:
            xo[c][b] = block[offsets[c]:offsets[c] + SIZES[c]]
    for b in range(4):
        block = xv[b, :, mine].T
        for c in chunks:
            xs[c][0, b] = block[offsets[c]:offsets[c] + SIZES[c]]
    pl.semaphore_wait(barrier, 23)

    rx = [net.copy(xo[c], xs[c].at[1], other, "c", bytes_of[c]) for c in chunks]
    ri = net.copy(idx_hbm, idx.at[1], other, "c", 4096)
    rt = net.copy(tiles_hbm, tiles.at[1], other, "c", 2**20)

    def g_slot(c, g):
        return lambda pp, k, lo, cnt: gs[c][g].at[pl.ds((pp * NZ + k) * 4 + lo, cnt)]

    group = (h, 1 - h)

    def d_slot(c, g):
        return lambda pp, k, lo, cnt: dg[c].at[pl.ds(((k * 2 + pp) * 2 + group[g]) * 4 + lo, cnt)]

    def multiply(c, g, source, at, side):
        def one(t, unused):
            product = dot(source[idx[g, at + 1, t]], tiles[g, idx[g, at, t]], 1, side)
            keep = idx[g, at + 2, t].astype(F32)
            sums[c][g * SLOTS + 1 + t] = product + keep * sums[c][g * SLOTS + t]
            return unused

        lax.fori_loop(0, NT, one, 0, unroll=4)
        net.now += MULTIPLY

    def forward_part(c, g):
        def part(pp, k, i):
            at = ((k * 2 + pp) * 2 + group[g]) * 4 + i
            return sums[c][idx[0, 3, at]] + sums[c][SLOTS + idx[1, 3, at]]

        return part

    def backward_part(c, g):
        return lambda pp, k, i: sums[c][g * SLOTS + idx[g, 7, (pp * NZ + k) * 4 + i]]

    issued_x = [None] * len(SIZES)

    def forward(c):
        if c:
            for e in issued_x[c - 1]:
                yield e
        events = []
        for g in (0, 1):
            if g == 1:
                yield rx[c]
            events.append(along_z[c].gather(PLAN_X[c][g], xs[c].at[g], g_slot(c, g), RANKS[0][0] + c, GATE_X))
            gs[c][g][pl.ds(row * 4, 4)] = xs[c][g]
        issued_x[c] = [e[0] for e in events]
        if c + 1 < len(SIZES):
            net.spawn(forward(c + 1), RANKS[0][0] + c + 1)
        if c == 0:
            for e in loads[1:3]:
                e.wait()
            yield ri
            yield rt
        for g in (0, 1):
            yield events[g][1]
            multiply(c, g, gs[c][g], 0, 1)
        dones = [
            along_x[c].scatter(PLAN_F[c][g], forward_part(c, g), fbufs[c][g], aggs[c].at[g], RANKS[0][1] + c - 0.5 * g)
            for g in (1, 0)
        ]
        yield dones[0]
        ra = net.copy(aggs[c].at[1], af[c].at[h], other, "c", bytes_of[c])
        yield dones[1]
        af[c][h] = aggs[c][0]
        yield ra

    def turn_weight():
        loads[3].wait()
        wt[...] = wv[...].T

    def turn_cotangent(i):
        def work():
            if i == 0:
                loads[4].wait()
            here = slice(i * TB, (i + 1) * TB)
            cott[:, here] = cotv[here, :].T

        return work

    net.fillers = [(0.4, turn_weight)] + [(0.4, turn_cotangent(i)) for i in range(4)]
    net.spawn(forward(0))
    net.run()

    agg = jnp.concatenate(
        [jnp.concatenate([af[c][e, b] for b in range(4)], axis=1) for e in (0, 1) for c in chunks], axis=0
    )
    pre = dot(wt[...], agg, 1, 0)
    sigma = jax.nn.sigmoid(pre)
    dpre = (cott[...].astype(F32) * sigma * (1.0 + pre * (1.0 - sigma))).astype(BF)
    dagg = dot(wv[...], dpre, 1, 0).astype(BF)
    for e in (0, 1):
        for c in chunks:
            for b in range(4):
                lo = e * TB + offsets[c]
                dall[c][e, b] = dagg[lo:lo + SIZES[c], b * TB:(b + 1) * TB]
    rd = [net.copy(dall[c].at[1 - h], ds[c].at[1], other, "c", bytes_of[c]) for c in chunks]
    for c in chunks:
        ds[c][0] = dall[c][h]
    act_ref[...] = (pre * sigma).astype(BF)
    issued_d = [None] * len(SIZES)

    def backward(c):
        if c:
            for e in issued_d[c - 1]:
                yield e
        events = []
        for g in (0, 1):
            if g == 1:
                yield rd[c]
            events.append(along_x[c].gather(PLAN_D[c][g], ds[c].at[g], d_slot(c, g), RANKS[1][0] + c, GATE_D))
            dg[c][pl.ds(chip * 8 + group[g] * 4, 4)] = ds[c][g]
        issued_d[c] = [e[0] for e in events]
        if c == 0:
            wpart[...] = dot(agg, dpre, 1, 1)
            net.now += 0.5
            net.spawn(weights(), 9)
        if c + 1 < len(SIZES):
            net.spawn(backward(c + 1), RANKS[1][0] + c + 1)
        for g in (0, 1):
            yield events[g][1]
        for g in (0, 1):
            multiply(c, g, dg[c], 4, 0)
        dones = [
            along_z[c].scatter(PLAN_B[c][g], backward_part(c, g), bbufs[c][g], fgs[c].at[g], RANKS[1][1] + c - 0.5 * g)
            for g in (1, 0)
        ]
        yield dones[0]
        rf = net.copy(fgs[c].at[1], fo[c].at[h], other, "c", bytes_of[c])
        yield dones[1]
        fo[c][h] = fgs[c][0]
        yield rf
        for e in (0, 1):
            lo = e * TB + offsets[c]
            for b in range(4):
                fg_ref[lo:lo + SIZES[c], b * TB:(b + 1) * TB] = fo[c][e, b]

    def weights():
        half = pl.ds(pl.multiple_of(h * TB, TB), TB)
        yield net.copy(wpart.at[pl.ds(pl.multiple_of((1 - h) * TB, TB), TB)], wpair, other, "c", 2**17)
        wpair[...] = wpair[...] + wpart[half]
        own = wpair[pl.ds(pl.multiple_of(row * 8, 8), 8)]
        wrow[row] = own
        cs = [
            net.copy(wpair.at[pl.ds(pl.multiple_of(d[0] * 8, 8), 8)], wrow.at[row], d, "w", 2**13) for d in mates
        ]
        for c in cs:
            yield c
        total = wrow[0]
        for i in range(1, 16):
            total = total + wrow[i]
        wmine[...] = total
        wcol[chip] = total
        cs = [net.copy(wmine, wcol.at[chip], d, "w", 2**13) for d in chips]
        for c in cs:
            yield c
        total = wcol[0]
        for i in range(1, 8):
            total = total + wcol[i]
        here = pl.ds(pl.multiple_of(h * TB + row * 8, 8), 8)
        wfull[here] = total
        cs = [net.copy(wfull.at[here], wfull.at[here], d, "w", 2**13) for d in mates]
        for c in cs:
            yield c
        yield net.copy(wfull.at[half], wfull.at[half], other, "c", 2**17)
        wg_ref[...] = wfull[...]

    net.spawn(backward(0))
    net.run()
    net.finish()


def write_order(coords_ref, order):
    i32 = jnp.int32
    lane = lax.broadcasted_iota(i32, (NT, TB), 1)
    down = lax.broadcasted_iota(i32, (NT, TB), 0)
    small = lax.broadcasted_iota(i32, (NT, NT), 1)
    pick = small == lax.broadcasted_iota(i32, (NT, NT), 0)

    def down_of(values):
        return jnp.sum(jnp.where(pick, values, 0), axis=1, keepdims=True)

    def along(chosen, values):
        return jnp.sum(jnp.where(chosen, values, 0), axis=0, keepdims=True)

    lanes = [jnp.broadcast_to(coords_ref[0, 0, i:i + 1, :], (NT, NT)) for i in (0, 1)]
    downs = [down_of(v) for v in lanes]
    for at, (a, b) in ((0, (0, 1)), (4, (1, 0))):
        key = lanes[a] * 64 + lanes[b]
        target, source = downs[a], downs[b]
        before = key < target * 64 + source
        rank = jnp.sum(jnp.where(before, 1, 0), axis=1, keepdims=True)
        placed = rank == lane
        now = along(placed, target)
        last = along(rank == lane - 1, target + 1) - 1
        order[at:at + 1, :] = along(placed, down)
        order[at + 1:at + 2, :] = along(placed, source)
        order[at + 2:at + 3, :] = jnp.where(now == last, 1, 0)
        upto = along(target <= lane, jnp.ones((NT, TB), i32))
        found = along(target == lane, jnp.ones((NT, TB), i32))
        order[at + 3:at + 4, :] = jnp.where(found > 0, upto, 0)


def turn(act_t, fg_t, wg_in, act_ref, fg_ref, wg_ref):
    for b in range(4):
        here = slice(b * TB, (b + 1) * TB)
        act_ref[here, :] = act_t[:, here].T
        fg_ref[here, :] = fg_t[:, here].T
    wg_ref[...] = wg_in[...]


def body(features, weight, cotangent, tiles, coords):
    vmem = pl.BlockSpec(memory_space=pltpu.VMEM)
    hbm = pl.BlockSpec(memory_space=pl.ANY)
    idx = pl.pallas_call(
        write_order,
        out_shape=jax.ShapeDtypeStruct((8, TB), jnp.int32),
        in_specs=[vmem],
        out_specs=vmem,
        name="order",
    )(coords)

    def units(c, *lead):
        return pltpu.VMEM((*lead, 4, SIZES[c], TB), BF)

    def each(*lead):
        return [units(c, *lead) for c in range(len(SIZES))]

    def sums_for(n, plan):
        m = n // 2
        shapes = {"a": ((2, 2, m), (2, 2, m), (), ()), "b": ((2, m), (2, m), (n,), (n,))}
        shapes |= {"e": ((2, n), (2, n), (), ()), "d": ((n,), (n,), (n,), (n,))}
        return [[[units(c, *t) for t in shapes[kind]] for kind in plan[c]] for c in range(len(SIZES))]

    def blocks():
        return [pltpu.VMEM((64, fc, TB), BF) for fc in SIZES]

    act, fg, wg = pl.pallas_call(
        kernel,
        out_shape=(
            jax.ShapeDtypeStruct((256, 512), BF),
            jax.ShapeDtypeStruct((256, 512), BF),
            jax.ShapeDtypeStruct((256, 256), F32),
        ),
        in_specs=[hbm] * 5,
        out_specs=(vmem, vmem, vmem),
        scratch_shapes=[
            pltpu.VMEM((4, TB, 256), BF),
            pltpu.VMEM((256, 256), BF),
            pltpu.VMEM((512, 256), BF),
            pltpu.VMEM((256, 256), BF),
            pltpu.VMEM((256, 512), BF),
            pltpu.VMEM((2, NT, TB, TB), BF),
            pltpu.SMEM((2, 8, TB), jnp.int32),
            each(),
            each(2),
            [list(pair) for pair in zip(blocks(), blocks())],
            [pltpu.VMEM((2 * SLOTS, fc, TB), F32) for fc in SIZES],
            each(2),
            each(2),
            each(2),
            each(2),
            blocks(),
            each(2),
            each(2),
            sums_for(NX, PLAN_F),
            sums_for(NZ, PLAN_B),
            pltpu.VMEM((256, 256), F32),
            pltpu.VMEM((128, 256), F32),
            pltpu.VMEM((16, 8, 256), F32),
            pltpu.VMEM((8, 256), F32),
            pltpu.VMEM((8, 8, 256), F32),
            pltpu.VMEM((256, 256), F32),
            pltpu.SemaphoreType.DMA((5,)),
            pltpu.SemaphoreType.DMA((SEMS,)),
            pltpu.SemaphoreType.DMA((SEMS,)),
        ],
        compiler_params=pltpu.CompilerParams(
            collective_id=0, has_side_effects=True, vmem_limit_bytes=56 * 2**20
        ),
        cost_estimate=pl.CostEstimate(flops=10**9, bytes_accessed=4 * 2**20, transcendentals=2**17),
        name="layer",
    )(features.reshape(4, TB, 256), weight, cotangent, tiles.reshape(NT, TB, TB), idx)
    return pl.pallas_call(
        turn,
        out_shape=(
            jax.ShapeDtypeStruct((512, 256), BF),
            jax.ShapeDtypeStruct((512, 256), BF),
            jax.ShapeDtypeStruct((256, 256), F32),
        ),
        in_specs=[vmem] * 3,
        out_specs=(vmem, vmem, vmem),
        name="turn",
    )(act, fg, wg)


def solution(mesh):
    return jax.shard_map(
        body,
        mesh=mesh,
        in_specs=(
            P(("col", "row"), None),
            P(),
            P(("row", "col"), None),
            P("row", "col", None, None, None),
            P("row", "col", None, None),
        ),
        out_specs=(P(("row", "col"), None), P(("col", "row"), None), P()),
        check_vma=False,
    )
```

```python
import jax
import jax.numpy as jnp
from jax import lax
from jax.experimental import pallas as pl
from jax.experimental.pallas import tpu as pltpu
from jax.sharding import PartitionSpec as P

MESH = pl.DeviceIdType.MESH
BF = jnp.bfloat16
F32 = jnp.float32
TB = 128
NT = 32
NZ = 8
NX = 4
SLOTS = NT + 1
SIZES = (80, 48)
PLAN_X = ('ab', 'ba')
PLAN_F = ('aa', 'ab')
PLAN_D = ("de","ee")
PLAN_B = ('ba', 'ba')
GATE_X = 2
GATE_D = 1
RANKS = ((0, 0), (0, 0))
SEMS = 320
INF = 1e9
LATE = {"c": 1.5, "y2": 2.7, "x2": 2.7, "w": 8.0, "z": 1.6}
RATE = 43.0
EMIT = 0.05
ISSUE = 0.08
MULTIPLY = 0.7


def dot(a, b, da, db):
    return lax.dot_general(a, b, (((da,), (db,)), ((), ())), preferred_element_type=F32)


def wrap(v, n):
    return lax.rem(v + n, n)


class Handle:
    def __init__(self, copy, left, eta):
        self.copy, self.left, self.eta = copy, left, eta
        self.waited = self.sent = False

    def wait(self):
        if not self.waited:
            self.copy.wait_recv()
            self.waited = True

    def wait_send(self):
        if not self.sent:
            self.copy.wait_send()
            self.sent = True


class Count:
    def __init__(self, net, need):
        self.net, self.need, self.eta = net, need, INF

    def hit(self):
        self.need -= 1
        if self.need == 0:
            self.eta = self.net.now

    def wait(self):
        pass


class Later:
    def __init__(self):
        self.handle = None

    @property
    def eta(self):
        return INF if self.handle is None else self.handle.eta

    def wait(self):
        self.handle.wait()


class Net:
    def __init__(self, send, recv):
        self.send, self.recv, self.used, self.started = send, recv, 0, []
        self.now, self.free, self.tasks, self.turn, self.fillers = 0.0, {}, [], 0, []

    def copy(self, src, dst, device, link, size):
        c = pltpu.make_async_remote_copy(
            src_ref=src,
            dst_ref=dst,
            send_sem=self.send.at[self.used],
            recv_sem=self.recv.at[self.used],
            device_id=device,
            device_id_type=MESH,
        )
        self.used += 1
        c.start()
        rate = 400.0 if link == "c" else RATE
        late = LATE.get(link, LATE["z"])
        names = {"y2": ("y",), "x2": ("x+", "x-")}.get(link, (link,))
        start = max([self.now] + [self.free.get(name, 0.0) for name in names])
        left = start + size / 1000.0 / rate
        for name in names:
            self.free[name] = left
        self.now += ISSUE
        handle = Handle(c, left, left + late)
        self.started.append(handle)
        return handle

    def spawn(self, task, rank=0):
        self.turn += 1
        self.tasks.append([task, None, rank, self.turn])

    def run(self):
        while self.tasks:
            best, key = None, None
            for t in self.tasks:
                eta = self.now if t[1] is None else max(t[1].eta, self.now)
                k = (eta, t[2], t[3])
                if key is None or k < key:
                    best, key = t, k
            assert key[0] < INF, "stuck"
            if key[0] - self.now > 0.6 and self.fillers:
                cost, work = self.fillers.pop(0)
                work()
                self.now += cost
                continue
            old = [e for e in self.started if not e.sent and e.left + 4.0 < self.now]
            for e in old[: max(0, int((key[0] - self.now) / 0.04))]:
                e.wait_send()
                self.now += 0.03
            self.now = max(self.now, key[0])
            if best[1] is not None:
                best[1].wait()
            self.turn += 1
            best[3] = self.turn
            try:
                best[1] = next(best[0])
            except StopIteration:
                self.tasks.remove(best)
        for cost, work in self.fillers:
            work()
        self.fillers = []

    def finish(self):
        for e in self.started:
            e.wait_send()


class Ring:
    def __init__(self, net, n, k, p, dev, axis, y, fc):
        self.net, self.n, self.m, self.k, self.p, self.q = net, n, n // 2, k, p, 1 - p
        self.dev, self.axis, self.y, self.fc = dev, axis, y, fc

    def side(self, d):
        return self.dev(wrap(self.k + 1, self.n) if d == 0 else wrap(self.k - 1, self.n), self.p)

    def ring(self, src, dst, d, cnt):
        return self.net.copy(src, dst, self.side(d), self.axis + "+-"[d], cnt * self.fc * TB * 2)

    def place(self, o):
        return (None, "x+", "x2", "x-")[o], self.dev(wrap(self.k + o, self.n), self.p)

    def straight(self, src, dst, o, cnt):
        link, device = self.place(o)
        return self.net.copy(src, dst, device, link, cnt * self.fc * TB * 2)

    def across(self, src, dst, cnt):
        return self.net.copy(src, dst, self.dev(self.k, self.q), self.y, cnt * self.fc * TB * 2)

    def gather(self, plan, own, slot, rank, gate):
        net, m, n, k, p, q = self.net, self.m, self.n, self.k, self.p, self.q
        if plan in "de":
            return self.gather_straight(plan, own, slot, rank)
        first = plan == "a"
        issued = Count(net, 4 if first else 2)
        done = Count(net, 4 if first else 2 * m + 3)

        def origin(d, s):
            return wrap(k - s, n) if d == 0 else wrap(k + s, n)

        def arrive(c):
            yield c
            done.hit()

        def over(o, lo, cnt, src):
            net.spawn(arrive(self.across(src, slot(p, o, lo, cnt), cnt)), rank)

        def chain(pp, d, src, c):
            if c is not None:
                yield c
            for s in range(1, m + 1):
                o = origin(d, s - 1)
                lo, cnt = (0, 4) if s < m else (2 * d, 2)
                here = slot(pp, o, lo, cnt) if s > 1 or src is None else src
                c = self.ring(here, slot(pp, o, lo, cnt), d, cnt)
                if s > 1 and not first:
                    over(o, 0, 4, slot(pp, o, 0, 4))
                if s == gate:
                    issued.hit()
                if s < m:
                    yield c
            yield c
            if not first:
                o = origin(d, m)
                over(o, 2 * d, 2, slot(pp, o, 2 * d, 2))
            done.hit()

        if first:
            ya = self.across(own, slot(p, k, 0, 4), 4)
            for d in (0, 1):
                net.spawn(chain(p, d, own, None), rank)
            for d in (0, 1):
                net.spawn(chain(q, d, None, ya), rank)
        else:
            for d in (0, 1):
                net.spawn(chain(p, d, own, None), rank)

            def start():
                yield None
                over(k, 0, 4, own)

            net.spawn(start(), rank)
        return issued, done

    def gather_straight(self, plan, own, slot, rank):
        net, n, k, p, q = self.net, self.n, self.k, self.p, self.q
        offsets = (2, 1, 3)
        issued = Count(net, 1)
        done = Count(net, 6 if plan == "e" else 4)

        def arrive(c):
            yield c
            done.hit()

        if plan == "e":
            ya = self.across(own, slot(p, k, 0, 4), 4)
            for o in offsets:
                net.spawn(arrive(self.straight(own, slot(p, k, 0, 4), o, 4)), rank)

            def onward():
                yield ya
                for o in offsets:
                    net.spawn(arrive(self.straight(slot(q, k, 0, 4), slot(q, k, 0, 4), o, 4)), rank)
                issued.hit()

            net.spawn(onward(), rank)
        else:
            net.spawn(arrive(self.across(own, slot(p, k, 0, 4), 4)), rank)
            came = {o: self.straight(own, slot(p, k, 0, 4), o, 4) for o in offsets}
            issued.hit()

            def onward(o):
                yield came[o]
                t = slot(p, wrap(k - o, n), 0, 4)
                net.spawn(arrive(self.across(t, t, 4)), rank)

            for o in offsets:
                net.spawn(onward(o), rank)
        return issued, done

    def scatter(self, plan, part, bufs, out, rank):
        net, m, n, k, p, q = self.net, self.m, self.n, self.k, self.p, self.q
        done = Count(net, 1)

        def emit(dst, lo, cnt, terms):
            def one(i, unused):
                total = terms[0](i)
                for t in terms[1:]:
                    total = total + t(i)
                dst[i] = total.astype(BF)
                return unused

            lax.fori_loop(lo, lo + cnt, one, 0, unroll=True)
            net.now += EMIT * cnt

        def read(ref):
            return lambda i: ref[i].astype(F32)

        def mine(pp, t):
            return lambda i: part(pp, t, i)

        def offset(d, s):
            return m + 1 - s if d == 0 else (n - (m + 1 - s)) % n

        def step(src, dst, d, s, terms, before):
            if s == 1:
                lo = 2 * d
                emit(src, lo, 2, terms)
                return self.ring(src.at[pl.ds(lo, 2)], dst.at[pl.ds(lo, 2)], d, 2)
            if s == 2:
                emit(src, 2 * d, 2, terms + [read(before)])
                emit(src, 2 - 2 * d, 2, terms)
            else:
                emit(src, 0, 4, terms + [read(before)])
            return self.ring(src, dst, d, 4)

        if plan in "de":
            offsets = (2, 1, 3)
        if plan == "e":
            sa, ra, sya, rya = bufs

            def final():
                came = {}
                for j, pp in ((0, q), (1, p)):
                    for o in offsets:
                        emit(sa.at[j, o], 0, 4, [mine(pp, wrap(k + o, n))])
                        came[j, o] = self.straight(sa.at[j, o], ra.at[j, o], o, 4)
                        yield None
                for o in offsets:
                    yield came[0, o]
                emit(sya, 0, 4, [mine(q, k)] + [read(ra.at[0, o]) for o in offsets])
                c = self.across(sya, rya, 4)
                for o in offsets:
                    yield came[1, o]
                yield c
                emit(out, 0, 4, [mine(p, k)] + [read(ra.at[1, o]) for o in offsets] + [read(rya)])
                done.hit()

            net.spawn(final(), rank)
        elif plan == "d":
            sb, rb, sy, ry = bufs

            def final():
                ys, came = {}, {}
                for o in offsets + (0,):
                    emit(sy.at[o], 0, 4, [mine(q, wrap(k + o, n))])
                    ys[o] = self.across(sy.at[o], ry.at[o], 4)
                    yield None
                for o in offsets:
                    yield ys[o]
                    emit(sb.at[o], 0, 4, [mine(p, wrap(k + o, n)), read(ry.at[o])])
                    came[o] = self.straight(sb.at[o], rb.at[o], o, 4)
                yield ys[0]
                for o in offsets:
                    yield came[o]
                emit(out, 0, 4, [mine(p, k), read(ry.at[0])] + [read(rb.at[o]) for o in offsets])
                done.hit()

            net.spawn(final(), rank)
        elif plan == "a":
            sa, ra, sya, rya = bufs
            rings = [Count(net, 2), Count(net, 2)]

            def chain(j, pp, d):
                for s in range(1, m + 1):
                    t = wrap(k + offset(d, s), n)
                    c = step(sa.at[j, d, s - 1], ra.at[j, d, s - 1], d, s, [mine(pp, t)], ra.at[j, d, max(s - 2, 0)])
                    yield c
                rings[j].hit()

            def last(j):
                return [read(ra.at[j, 0, m - 1]), read(ra.at[j, 1, m - 1])]

            def final():
                yield rings[0]
                emit(sya, 0, 4, [mine(q, k)] + last(0))
                c = self.across(sya, rya, 4)
                yield rings[1]
                yield c
                emit(out, 0, 4, [mine(p, k)] + last(1) + [read(rya)])
                done.hit()

            for j, pp in ((0, q), (1, p)):
                for d in (0, 1):
                    net.spawn(chain(j, pp, d), rank)
            net.spawn(final(), rank)
        else:
            sb, rb, sy, ry = bufs
            ys = [Later() for i in range(n)]
            rings = Count(net, 2)

            def send():
                order = [m]
                for s in range(2, m + 1):
                    order += [offset(0, s), offset(1, s)]
                for o in order + [0]:
                    emit(sy.at[o], 0, 4, [mine(q, wrap(k + o, n))])
                    ys[o].handle = self.across(sy.at[o], ry.at[o], 4)
                    yield None

            def chain(d):
                for s in range(1, m + 1):
                    o = offset(d, s)
                    yield ys[o]
                    terms = [mine(p, wrap(k + o, n)), read(ry.at[o])]
                    c = step(sb.at[d, s - 1], rb.at[d, s - 1], d, s, terms, rb.at[d, max(s - 2, 0)])
                    yield c
                rings.hit()

            def final():
                yield rings
                yield ys[0]
                emit(out, 0, 4, [mine(p, k), read(ry.at[0]), read(rb.at[0, m - 1]), read(rb.at[1, m - 1])])
                done.hit()

            net.spawn(send(), rank)
            for d in (0, 1):
                net.spawn(chain(d), rank)
            net.spawn(final(), rank)
        return done


def kernel(
    x_hbm, w_hbm, cot_hbm, tiles_hbm, idx_hbm, act_ref, fg_ref, wg_ref,
    xv, wv, cotv, wt, cott, tiles, idx, xo, xs, gs, sums, aggs, af, dall, ds, dg, fgs, fo,
    fbufs, bbufs, wpart, wpair, wrow, wmine, wcol, wfull,
    local, send, recv,
):
    row, col = lax.axis_index("row"), lax.axis_index("col")
    p, z = lax.div(row, NZ), lax.rem(row, NZ)
    h = lax.rem(col, 2)
    chip = lax.div(col, 2)
    x, u = lax.div(chip, 2), lax.rem(chip, 2)
    other = (row, col + 1 - 2 * h)
    net = Net(send, recv)
    along_z = [Ring(net, NZ, z, p, lambda k, pp: (pp * NZ + k, col), "z", "y", fc) for fc in SIZES]
    along_x = [Ring(net, NX, x, u, lambda k, pp: (row, (k * 2 + pp) * 2 + h), "x", "y2", fc) for fc in SIZES]
    mates = [(wrap(row + d, 16), col) for d in range(1, 16)]
    chips = [(row, wrap(chip + d, 8) * 2 + h) for d in range(1, 8)]
    chunks = range(len(SIZES))
    offsets = [sum(SIZES[:c]) for c in chunks]
    bytes_of = [4 * fc * TB * 2 for fc in SIZES]

    barrier = pltpu.get_barrier_semaphore()
    for device in mates + chips + [other]:
        pl.semaphore_signal(barrier, inc=1, device_id=device, device_id_type=MESH)

    pairs = ((x_hbm, xv), (idx_hbm, idx.at[0]), (tiles_hbm, tiles.at[0]), (w_hbm, wv), (cot_hbm, cotv))
    loads = [pltpu.make_async_copy(a, b, local.at[i]) for i, (a, b) in enumerate(pairs)]
    for c in loads:
        c.start()
    for c in chunks:
        sums[c][0] = jnp.zeros((SIZES[c], TB), F32)
        sums[c][SLOTS] = jnp.zeros((SIZES[c], TB), F32)

    mine = pl.ds(pl.multiple_of(h * TB, TB), TB)
    theirs = pl.ds(pl.multiple_of((1 - h) * TB, TB), TB)
    loads[0].wait()
    for b in range(4):
        block = xv[b, :, theirs].T
        for c in chunks:
            xo[c][b] = block[offsets[c]:offsets[c] + SIZES[c]]
    for b in range(4):
        block = xv[b, :, mine].T
        for c in chunks:
            xs[c][0, b] = block[offsets[c]:offsets[c] + SIZES[c]]
    pl.semaphore_wait(barrier, 23)

    rx = [net.copy(xo[c], xs[c].at[1], other, "c", bytes_of[c]) for c in chunks]
    ri = net.copy(idx_hbm, idx.at[1], other, "c", 4096)
    rt = net.copy(tiles_hbm, tiles.at[1], other, "c", 2**20)

    def g_slot(c, g):
        return lambda pp, k, lo, cnt: gs[c][g].at[pl.ds((pp * NZ + k) * 4 + lo, cnt)]

    group = (h, 1 - h)

    def d_slot(c, g):
        return lambda pp, k, lo, cnt: dg[c].at[pl.ds(((k * 2 + pp) * 2 + group[g]) * 4 + lo, cnt)]

    def multiply(c, g, source, at, side):
        def one(t, unused):
            product = dot(source[idx[g, at + 1, t]], tiles[g, idx[g, at, t]], 1, side)
            keep = idx[g, at + 2, t].astype(F32)
            sums[c][g * SLOTS + 1 + t] = product + keep * sums[c][g * SLOTS + t]
            return unused

        lax.fori_loop(0, NT, one, 0, unroll=8)
        net.now += MULTIPLY

    def forward_part(c, g):
        def part(pp, k, i):
            at = ((k * 2 + pp) * 2 + group[g]) * 4 + i
            return sums[c][idx[0, 3, at]] + sums[c][SLOTS + idx[1, 3, at]]

        return part

    def backward_part(c, g):
        return lambda pp, k, i: sums[c][g * SLOTS + idx[g, 7, (pp * NZ + k) * 4 + i]]

    issued_x = [None] * len(SIZES)

    def forward(c):
        if c:
            for e in issued_x[c - 1]:
                yield e
        events = []
        for g in (0, 1):
            if g == 1:
                yield rx[c]
            events.append(along_z[c].gather(PLAN_X[c][g], xs[c].at[g], g_slot(c, g), RANKS[0][0] + c, GATE_X))
            gs[c][g][pl.ds(row * 4, 4)] = xs[c][g]
        issued_x[c] = [e[0] for e in events]
        if c + 1 < len(SIZES):
            net.spawn(forward(c + 1), RANKS[0][0] + c + 1)
        if c == 0:
            for e in loads[1:3]:
                e.wait()
            yield ri
            yield rt
        for g in (0, 1):
            yield events[g][1]
            multiply(c, g, gs[c][g], 0, 1)
        dones = [
            along_x[c].scatter(PLAN_F[c][g], forward_part(c, g), fbufs[c][g], aggs[c].at[g], RANKS[0][1] + c - 0.5 * g)
            for g in (1, 0)
        ]
        yield dones[0]
        ra = net.copy(aggs[c].at[1], af[c].at[h], other, "c", bytes_of[c])
        yield dones[1]
        af[c][h] = aggs[c][0]
        yield ra

    def turn_weight():
        loads[3].wait()
        wt[...] = wv[...].T

    def turn_cotangent(i):
        def work():
            if i == 0:
                loads[4].wait()
            here = slice(i * TB, (i + 1) * TB)
            cott[:, here] = cotv[here, :].T

        return work

    net.fillers = [(0.4, turn_weight)] + [(0.4, turn_cotangent(i)) for i in range(4)]
    net.spawn(forward(0))
    net.run()

    agg = jnp.concatenate(
        [jnp.concatenate([af[c][e, b] for b in range(4)], axis=1) for e in (0, 1) for c in chunks], axis=0
    )
    pre = dot(wt[...], agg, 1, 0)
    sigma = jax.nn.sigmoid(pre)
    dpre = (cott[...].astype(F32) * sigma * (1.0 + pre * (1.0 - sigma))).astype(BF)
    dagg = dot(wv[...], dpre, 1, 0).astype(BF)
    for e in (0, 1):
        for c in chunks:
            for b in range(4):
                lo = e * TB + offsets[c]
                dall[c][e, b] = dagg[lo:lo + SIZES[c], b * TB:(b + 1) * TB]
    rd = [net.copy(dall[c].at[1 - h], ds[c].at[1], other, "c", bytes_of[c]) for c in chunks]
    for c in chunks:
        ds[c][0] = dall[c][h]
    act_ref[...] = (pre * sigma).astype(BF)
    issued_d = [None] * len(SIZES)

    def backward(c):
        if c:
            for e in issued_d[c - 1]:
                yield e
        events = []
        for g in (0, 1):
            if g == 1:
                yield rd[c]
            events.append(along_x[c].gather(PLAN_D[c][g], ds[c].at[g], d_slot(c, g), RANKS[1][0] + c, GATE_D))
            dg[c][pl.ds(chip * 8 + group[g] * 4, 4)] = ds[c][g]
        issued_d[c] = [e[0] for e in events]
        if c == 0:
            wpart[...] = dot(agg, dpre, 1, 1)
            net.now += 0.5
            net.spawn(weights(), 9)
        if c + 1 < len(SIZES):
            net.spawn(backward(c + 1), RANKS[1][0] + c + 1)
        for g in (0, 1):
            yield events[g][1]
        for g in (0, 1):
            multiply(c, g, dg[c], 4, 0)
        dones = [
            along_z[c].scatter(PLAN_B[c][g], backward_part(c, g), bbufs[c][g], fgs[c].at[g], RANKS[1][1] + c - 0.5 * g)
            for g in (1, 0)
        ]
        yield dones[0]
        rf = net.copy(fgs[c].at[1], fo[c].at[h], other, "c", bytes_of[c])
        yield dones[1]
        fo[c][h] = fgs[c][0]
        yield rf
        for e in (0, 1):
            lo = e * TB + offsets[c]
            for b in range(4):
                fg_ref[lo:lo + SIZES[c], b * TB:(b + 1) * TB] = fo[c][e, b]

    def weights():
        half = pl.ds(pl.multiple_of(h * TB, TB), TB)
        yield net.copy(wpart.at[pl.ds(pl.multiple_of((1 - h) * TB, TB), TB)], wpair, other, "c", 2**17)
        wpair[...] = wpair[...] + wpart[half]
        own = wpair[pl.ds(pl.multiple_of(row * 8, 8), 8)]
        wrow[row] = own
        cs = [
            net.copy(wpair.at[pl.ds(pl.multiple_of(d[0] * 8, 8), 8)], wrow.at[row], d, "w", 2**13) for d in mates
        ]
        for c in cs:
            yield c
        total = wrow[0]
        for i in range(1, 16):
            total = total + wrow[i]
        wmine[...] = total
        wcol[chip] = total
        cs = [net.copy(wmine, wcol.at[chip], d, "w", 2**13) for d in chips]
        for c in cs:
            yield c
        total = wcol[0]
        for i in range(1, 8):
            total = total + wcol[i]
        here = pl.ds(pl.multiple_of(h * TB + row * 8, 8), 8)
        wfull[here] = total
        cs = [net.copy(wfull.at[here], wfull.at[here], d, "w", 2**13) for d in mates]
        for c in cs:
            yield c
        yield net.copy(wfull.at[half], wfull.at[half], other, "c", 2**17)
        wg_ref[...] = wfull[...]

    net.spawn(backward(0))
    net.run()
    net.finish()


def write_order(coords_ref, order):
    i32 = jnp.int32
    lane = lax.broadcasted_iota(i32, (NT, TB), 1)
    down = lax.broadcasted_iota(i32, (NT, TB), 0)
    small = lax.broadcasted_iota(i32, (NT, NT), 1)
    pick = small == lax.broadcasted_iota(i32, (NT, NT), 0)

    def down_of(values):
        return jnp.sum(jnp.where(pick, values, 0), axis=1, keepdims=True)

    def along(chosen, values):
        return jnp.sum(jnp.where(chosen, values, 0), axis=0, keepdims=True)

    lanes = [jnp.broadcast_to(coords_ref[0, 0, i:i + 1, :], (NT, NT)) for i in (0, 1)]
    downs = [down_of(v) for v in lanes]
    for at, (a, b) in ((0, (0, 1)), (4, (1, 0))):
        key = lanes[a] * 64 + lanes[b]
        target, source = downs[a], downs[b]
        before = key < target * 64 + source
        rank = jnp.sum(jnp.where(before, 1, 0), axis=1, keepdims=True)
        placed = rank == lane
        now = along(placed, target)
        last = along(rank == lane - 1, target + 1) - 1
        order[at:at + 1, :] = along(placed, down)
        order[at + 1:at + 2, :] = along(placed, source)
        order[at + 2:at + 3, :] = jnp.where(now == last, 1, 0)
        upto = along(target <= lane, jnp.ones((NT, TB), i32))
        found = along(target == lane, jnp.ones((NT, TB), i32))
        order[at + 3:at + 4, :] = jnp.where(found > 0, upto, 0)


def turn(act_t, fg_t, wg_in, act_ref, fg_ref, wg_ref):
    for b in range(4):
        here = slice(b * TB, (b + 1) * TB)
        act_ref[here, :] = act_t[:, here].T
        fg_ref[here, :] = fg_t[:, here].T
    wg_ref[...] = wg_in[...]


def body(features, weight, cotangent, tiles, coords):
    vmem = pl.BlockSpec(memory_space=pltpu.VMEM)
    hbm = pl.BlockSpec(memory_space=pl.ANY)
    idx = pl.pallas_call(
        write_order,
        out_shape=jax.ShapeDtypeStruct((8, TB), jnp.int32),
        in_specs=[vmem],
        out_specs=vmem,
        name="order",
    )(coords)

    def units(c, *lead):
        return pltpu.VMEM((*lead, 4, SIZES[c], TB), BF)

    def each(*lead):
        return [units(c, *lead) for c in range(len(SIZES))]

    def sums_for(n, plan):
        m = n // 2
        shapes = {"a": ((2, 2, m), (2, 2, m), (), ()), "b": ((2, m), (2, m), (n,), (n,))}
        shapes |= {"e": ((2, n), (2, n), (), ()), "d": ((n,), (n,), (n,), (n,))}
        return [[[units(c, *t) for t in shapes[kind]] for kind in plan[c]] for c in range(len(SIZES))]

    def blocks():
        return [pltpu.VMEM((64, fc, TB), BF) for fc in SIZES]

    act, fg, wg = pl.pallas_call(
        kernel,
        out_shape=(
            jax.ShapeDtypeStruct((256, 512), BF),
            jax.ShapeDtypeStruct((256, 512), BF),
            jax.ShapeDtypeStruct((256, 256), F32),
        ),
        in_specs=[hbm] * 5,
        out_specs=(vmem, vmem, vmem),
        scratch_shapes=[
            pltpu.VMEM((4, TB, 256), BF),
            pltpu.VMEM((256, 256), BF),
            pltpu.VMEM((512, 256), BF),
            pltpu.VMEM((256, 256), BF),
            pltpu.VMEM((256, 512), BF),
            pltpu.VMEM((2, NT, TB, TB), BF),
            pltpu.SMEM((2, 8, TB), jnp.int32),
            each(),
            each(2),
            [list(pair) for pair in zip(blocks(), blocks())],
            [pltpu.VMEM((2 * SLOTS, fc, TB), F32) for fc in SIZES],
            each(2),
            each(2),
            each(2),
            each(2),
            blocks(),
            each(2),
            each(2),
            sums_for(NX, PLAN_F),
            sums_for(NZ, PLAN_B),
            pltpu.VMEM((256, 256), F32),
            pltpu.VMEM((128, 256), F32),
            pltpu.VMEM((16, 8, 256), F32),
            pltpu.VMEM((8, 256), F32),
            pltpu.VMEM((8, 8, 256), F32),
            pltpu.VMEM((256, 256), F32),
            pltpu.SemaphoreType.DMA((5,)),
            pltpu.SemaphoreType.DMA((SEMS,)),
            pltpu.SemaphoreType.DMA((SEMS,)),
        ],
        compiler_params=pltpu.CompilerParams(
            collective_id=0, has_side_effects=True, vmem_limit_bytes=56 * 2**20
        ),
        cost_estimate=pl.CostEstimate(flops=10**9, bytes_accessed=4 * 2**20, transcendentals=2**17),
        name="layer",
    )(features.reshape(4, TB, 256), weight, cotangent, tiles.reshape(NT, TB, TB), idx)
    return pl.pallas_call(
        turn,
        out_shape=(
            jax.ShapeDtypeStruct((512, 256), BF),
            jax.ShapeDtypeStruct((512, 256), BF),
            jax.ShapeDtypeStruct((256, 256), F32),
        ),
        in_specs=[vmem] * 3,
        out_specs=(vmem, vmem, vmem),
        name="turn",
    )(act, fg, wg)


def solution(mesh):
    return jax.shard_map(
        body,
        mesh=mesh,
        in_specs=(
            P(("col", "row"), None),
            P(),
            P(("row", "col"), None),
            P("row", "col", None, None, None),
            P("row", "col", None, None),
        ),
        out_specs=(P(("row", "col"), None), P(("col", "row"), None), P()),
        check_vma=False,
    )
```
